32 devices in a mesh: row: 8 (over z, y), col: 4 (over x, core).
Axes of the slice: x: 2, y: 2, z: 4, core: 2. Of those that a mesh axis runs over, the one named last changes fastest.
Arguments:
- rhs: float32 [2, 4096, 4096], P(None, 'row', 'col'), may hold values from -6 to 6
- factor: float32 [2, 4096, 1024], P(None, 'row', 'col'), may hold values from -0.1875 to 0.1875
- inverses: float32 [2, 512, 512], replicated, may hold values from -1 to 3, as said below
Outputs:
- updated: float32 [2, 4096, 4096], P(None, 'row', 'col')
The draws below stay inside these ranges and needn't reach their ends.
Inputs may be any that keep to these rules, and one draw needn't show every extreme that they name: `inverses`: each inverse is lower triangular with a diagonal between 0.3 and 3.
All inputs are finite; a program needn't handle non-finite values.
Results may differ from the reference program's by a relative error of at most 0.000064.
Values sent between devices are 32-bit elements; how exact they have to be, the bound alone decides.
A program may use at most 128 MiB of HBM per device.

```python
import jax
import jax.numpy as jnp
from jax import lax

NB = 512
BPD = 2
R = 4096
N_ROW = 8


def draw_inverses(key, part):
    key = jax.random.fold_in(key, 7)
    key_off, key_diag = jax.random.split(key)
    off_part = jnp.clip(jax.random.normal(key_off, (2, NB, NB), jnp.float32), -6.0, 6.0) * NB ** (-0.5)
    lower = jnp.tril(off_part, -1)
    diag_part = jax.random.uniform(key_diag, (2, NB), jnp.float32, 0.5, 1.5)
    eye_table = jnp.eye(NB, dtype=jnp.float32)
    return lower + diag_part[:, :, None] * eye_table[None, :, :]


def block_levels(stream_key, dims, cuts, least, high):
    def one(axis_at, parts):
        heights = jax.random.uniform(jax.random.fold_in(jax.random.fold_in(stream_key, 6), axis_at), (parts,), jnp.float32, least / len(cuts), high / len(cuts))
        return jnp.repeat(jnp.exp(heights), dims[axis_at] // parts).reshape((-1,) + (1,) * (len(dims) - axis_at - 1))

    level = one(*cuts[0])
    for cut in cuts[1:]:
        level = level * one(*cut)
    return level


def noise(key, dims, deviation, limit, pieces=(), kind=jnp.bfloat16):
    values = deviation * jax.random.normal(key, dims, jnp.float32)
    if pieces:
        values = values * block_levels(key, dims, pieces, -0.22, 0.18)
    return jnp.clip(values, -limit, limit).astype(kind)


def setup_inputs(seed: int = 0) -> dict:
    key_of = jax.random.split(jax.random.key(seed), 4)
    return {
        "rhs": noise(key_of[0], (BPD, N_ROW * NB, R), 1.0, 6.0, ((1, 8), (2, 4)), jnp.float32),
        "factor": noise(key_of[1], (BPD, N_ROW * NB, 2 * NB), (2 * NB) ** -0.5, 0.1875, ((1, 8), (2, 4)), jnp.float32),
        "inverses": draw_inverses(jax.random.fold_in(key_of[3], 71), 0),
    }


def reference(rhs, factor, inverses):
    highest = lax.Precision.HIGHEST
    blocks = rhs.reshape(BPD, N_ROW, NB, R)
    panel = factor.reshape(BPD, N_ROW, NB, 2 * NB)
    first = jnp.dot(inverses[0], blocks[0, 0], precision=highest, preferred_element_type=jnp.float32)
    after_first = blocks - jnp.einsum("jrtk,kc->jrtc", panel[..., :NB], first, precision=highest)
    second = jnp.dot(inverses[1], after_first[0, 1], precision=highest, preferred_element_type=jnp.float32)
    result = after_first - jnp.einsum("jrtk,kc->jrtc", panel[..., NB:], second, precision=highest)
    result = result.at[0, 0].set(first).at[0, 1].set(second)
    return result.reshape(rhs.shape)
```

```python
import functools

import jax
import jax.numpy as jnp
from jax import lax
from jax.experimental import pallas as pl
from jax.experimental.pallas import tpu as pltpu
from jax.sharding import PartitionSpec as P

MESH = pl.DeviceIdType.MESH
CW = 256
PR = 64
WINDOW = 4


def split(value):
    high = value.astype(jnp.bfloat16)
    low = (value - high.astype(jnp.float32)).astype(jnp.bfloat16)
    return high, low


def dot3(ah, al, bh, bl):
    def one(a, b):
        return jnp.dot(a, b, preferred_element_type=jnp.float32)

    return one(ah, bh) + one(al, bh) + one(ah, bl)


def kernel(n_row, rhs, fac, inv, out, acc, lane, pan, l10p, invf, ph, plo, ih, il, lh, ll, xh, xl, bh, bl, f32s, s32s,
           acc_sem, inv_sem, own_sem, out_sem, zs, zr, ys, yr, xs, xr, ps, pr, ts, tr, ls, lr):
    nb = rhs.shape[1]
    n_chunk = rhs.shape[2] // CW
    ppc = nb // PR
    n_l = ppc // 2
    n_piece = n_chunk * ppc + n_l
    l_at = 2 * ppc
    half = nb // 2

    r = lax.axis_index("row")
    c = lax.axis_index("col")
    z, y = r // 2, r % 2
    n_z = n_row // 2
    core = c % 2
    partner = c + 1 - 2 * core
    peer = (c + 2) % 4
    peer2 = (partner + 2) % 4
    has_up = z < n_z - 1
    has_down = z > 0
    up, down, across = (r + 2, c), (r - 2, c), (r + 1 - 2 * y, c)
    beside, far = (r, partner), (r, peer)

    def base(k):
        return k * ppc + jnp.where(k >= 2, n_l, 0)

    def load_acc(k, j):
        return pltpu.make_async_copy(
            rhs.at[j, :, pl.ds(k * CW, CW)], acc.at[k, pl.ds(j * nb, nb)], acc_sem.at[k, j])

    for k in range(n_chunk):
        load_acc(k, 0).start()
    own = [pltpu.make_async_copy(fac.at[j], pan.at[c, j], own_sem.at[j]) for j in range(2)]
    inv_copy = [pltpu.make_async_copy(inv.at[i], invf.at[i], inv_sem.at[i]) for i in range(2)]
    for copy in own + inv_copy:
        copy.start()
    for k in range(n_chunk):
        load_acc(k, 1).start()

    barrier = pltpu.get_barrier_semaphore()
    for there in (across, beside, far):
        pl.semaphore_signal(barrier, inc=1, device_id=there, device_id_type=MESH)

    @pl.when(has_up)
    def _():
        pl.semaphore_signal(barrier, inc=1, device_id=up, device_id_type=MESH)

    @pl.when(has_down)
    def _():
        pl.semaphore_signal(barrier, inc=1, device_id=down, device_id_type=MESH)

    pl.semaphore_wait(barrier, 3 + has_up.astype(jnp.int32) + has_down.astype(jnp.int32))

    def remote(src, dst, ssem, rsem, there):
        return pltpu.make_async_remote_copy(
            src_ref=src, dst_ref=dst, send_sem=ssem, recv_sem=rsem, device_id=there, device_id_type=MESH)

    def z_copy(p):
        return remote(lane.at[y, p], lane.at[y, p], zs.at[p], zr.at[p], up)

    def y_copy(p):
        return remote(lane.at[y, p], lane.at[y, p], ys.at[p], yr.at[p], across)

    def y_arrival(p):
        return remote(lane.at[1 - y, p], lane.at[1 - y, p], ys.at[p], yr.at[p], across)

    def x_copy(j):
        return remote(fac.at[j], pan.at[c, j], xs.at[j], xr.at[j], far)

    def x_arrival(j):
        return remote(fac.at[j], pan.at[peer, j], xs.at[j], xr.at[j], far)

    def p_copy(i):
        if i < 2:
            return remote(fac.at[i], pan.at[c, i], ps.at[i], pr.at[i], beside)
        return remote(pan.at[peer, i - 2], pan.at[peer, i - 2], ps.at[i], pr.at[i], beside)

    def p_arrival(i):
        at = partner if i < 2 else peer2
        return remote(pan.at[at, i % 2], pan.at[at, i % 2], ps.at[i], pr.at[i], beside)

    def t_copy(i):
        return remote(pan.at[core, 0, pl.ds(i * PR, PR)], lane.at[0, l_at + i], ts.at[i], tr.at[i], across)

    def l_copy(b):
        return remote(lane.at[b, pl.ds(l_at, n_l)], l10p.at[b], ls.at[b], lr.at[b], beside)

    def relay(p):
        @pl.when(has_down)
        def _():
            z_copy(p).wait_recv()

        @pl.when(jnp.logical_and(z == 0, p >= WINDOW))
        def _():
            y_copy(p - WINDOW).wait_send()

            @pl.when(has_up)
            def _():
                z_copy(p - WINDOW).wait_send()

        @pl.when(has_up)
        def _():
            z_copy(p).start()

        y_copy(p).start()

    def relays(start, stop):
        @pl.loop(start, stop)
        def _(p):
            relay(p)

    def fill(k):
        load_acc(k, 0).wait()

        @pl.when(z == 0)
        def _():
            at = k * ppc + (n_l if k >= 2 else 0)
            lane[y, pl.ds(at, ppc)] = acc[k, pl.ds(0, nb)].reshape(ppc, PR, CW)

    x_copy(0).start()
    p_copy(0).start()
    p_copy(1).start()
    fill(0)
    relays(0, 3)
    for k in range(1, n_chunk):
        fill(k)
    relays(3, 5)
    inv_copy[0].wait()
    ih[0], il[0] = split(invf[0])
    relays(5, 7)
    inv_copy[1].wait()
    ih[1], il[1] = split(invf[1])
    relays(7, 8)

    x_arrival(0).wait_recv()
    p_copy(2).start()
    x_copy(1).start()
    for copy in own:
        copy.wait()

    @pl.when(r == 1)
    def _():
        for i in range(n_l):
            t_copy(i).start()
        lane[1, pl.ds(l_at, n_l)] = pan[core, 0, pl.ds(half, half)].reshape(n_l, PR, CW)

    relays(8, 12)
    p_arrival(0).wait_recv()
    p_arrival(1).wait_recv()
    p_arrival(2).wait_recv()

    def split_panel(q, j):
        h, l = split(pan[q, j])
        ph[pl.ds(j * nb, nb), pl.ds(q * CW, CW)] = h
        plo[pl.ds(j * nb, nb), pl.ds(q * CW, CW)] = l

    for q in range(4):
        relay(12 + q)
        split_panel(q, 0)

    @pl.when(r == 0)
    def _():
        for i in range(n_l):
            t_copy(i).wait_recv()

    relays(16, 18)
    x_arrival(1).wait_recv()
    p_copy(3).start()
    relays(18, 21)
    for i in range(n_l):
        y_arrival(l_at + i).wait_recv()
    for b in range(2):
        l_copy(b).start()
    p_arrival(3).wait_recv()
    for q in range(4):
        if q:
            relay(20 + q)
        split_panel(q, 1)
    for b in range(2):
        l_copy(b).wait_recv()
        for at, block in ((core, lane[b, pl.ds(l_at, n_l)]), (1 - core, l10p[b])):
            h, l = split(block.reshape(half, CW))
            lh[at, pl.ds(b * half, half)] = h
            ll[at, pl.ds(b * half, half)] = l
    for k in range(n_chunk):
        load_acc(k, 1).wait()

    def triangle(i, m):
        rows, cols = slice(m * half, (m + 1) * half), slice(0, (m + 1) * half)
        return dot3(ih[i, rows, cols], il[i, rows, cols], bh[cols], bl[cols])

    def solve(k):
        @pl.loop(base(k), base(k) + ppc)
        def _(p):
            y_arrival(p).wait_recv()

        bh[...], bl[...] = split(lane[0, pl.ds(base(k), ppc)].reshape(nb, CW))
        for m in range(2):
            rows = slice(m * half, (m + 1) * half)
            part = triangle(0, m)
            f32s[rows] = part
            xh[rows], xl[rows] = split(part)
        for m in range(2):
            rows = slice(m * half, (m + 1) * half)
            b1 = lane[1, pl.ds(base(k) + m * n_l, n_l)].reshape(half, CW)
            part = b1
            for q in range(2):
                ks = slice(q * half, (q + 1) * half)
                part = part - dot3(lh[q, rows], ll[q, rows], xh[ks], xl[ks])
            bh[rows], bl[rows] = split(part)
        for m in range(2):
            rows = slice(m * half, (m + 1) * half)
            at = slice(nb + m * half, nb + (m + 1) * half)
            part = triangle(1, m)
            s32s[rows] = part
            xh[at], xl[at] = split(part)

    def out_copy(k, t):
        return pltpu.make_async_copy(
            acc.at[k, pl.ds(pl.multiple_of(t * half, half), half)],
            out.at[t // 2, pl.ds(pl.multiple_of((t % 2) * half, half), half),
                   pl.ds(pl.multiple_of(k * CW, CW), CW)],
            out_sem.at[k, t])

    def update(k, t):
        rows = pl.ds(pl.multiple_of(t * half, half), half)
        solved = jnp.logical_and(r < 2, t < 2)

        @pl.when(jnp.logical_not(solved))
        def _():
            acc[k, rows] = acc[k, rows] - dot3(ph[rows], plo[rows], xh[...], xl[...])

        @pl.when(jnp.logical_and(solved, r == 0))
        def _():
            acc[k, rows] = f32s[rows]

        @pl.when(jnp.logical_and(solved, r == 1))
        def _():
            acc[k, rows] = s32s[rows]

        out_copy(k, t).start()

    def substep(n):
        k, u = n // 5, n % 5

        @pl.when(u == 0)
        def _():
            solve(k)

        @pl.when(u > 0)
        def _():
            update(k, u - 1)

    lead = 5 * (n_chunk - 1)

    @pl.loop(0, 20)
    def _(n):
        @pl.when(jnp.logical_and(n < 16, n % 2 == 0))
        def _():
            relay(24 + n // 2)

        @pl.when(n == lead)
        def _():
            relays(32, n_piece)

        substep(n)

    x_copy(0).wait_send()
    x_copy(1).wait_send()
    for i in range(4):
        p_copy(i).wait_send()
    for b in range(2):
        l_copy(b).wait_send()

    @pl.when(r == 1)
    def _():
        for i in range(n_l):
            t_copy(i).wait_send()

    @pl.loop(jnp.where(z == 0, n_piece - WINDOW, 0), n_piece)
    def _(p):
        y_copy(p).wait_send()

        @pl.when(has_up)
        def _():
            z_copy(p).wait_send()

    @pl.loop(0, n_chunk)
    def _(k):
        for t in range(4):
            out_copy(k, t).wait()


def shards(n_row, rhs, factor, inverses):
    nb = rhs.shape[1]
    n_chunk = rhs.shape[2] // CW
    ppc = nb // PR
    n_l = ppc // 2
    n_piece = n_chunk * ppc + n_l
    f32, bf16, dma = jnp.float32, jnp.bfloat16, pltpu.SemaphoreType.DMA
    anywhere = pl.BlockSpec(memory_space=pl.ANY)
    return pl.pallas_call(
        functools.partial(kernel, n_row),
        out_shape=jax.ShapeDtypeStruct(rhs.shape, f32),
        in_specs=[anywhere] * 3,
        out_specs=anywhere,
        scratch_shapes=[
            pltpu.VMEM((n_chunk, 2 * nb, CW), f32),
            pltpu.VMEM((2, n_piece, PR, CW), f32),
            pltpu.VMEM((4, 2, nb, CW), f32),
            pltpu.VMEM((2, n_l, PR, CW), f32),
            pltpu.VMEM((2, nb, nb), f32),
            pltpu.VMEM((2 * nb, 2 * nb), bf16),
            pltpu.VMEM((2 * nb, 2 * nb), bf16),
            pltpu.VMEM((2, nb, nb), bf16),
            pltpu.VMEM((2, nb, nb), bf16),
            pltpu.VMEM((2, nb, CW), bf16),
            pltpu.VMEM((2, nb, CW), bf16),
            pltpu.VMEM((2 * nb, CW), bf16),
            pltpu.VMEM((2 * nb, CW), bf16),
            pltpu.VMEM((nb, CW), bf16),
            pltpu.VMEM((nb, CW), bf16),
            pltpu.VMEM((nb, CW), f32),
            pltpu.VMEM((nb, CW), f32),
            dma((n_chunk, 2)), dma((2,)), dma((2,)), dma((n_chunk, 4)),
            dma((n_piece,)), dma((n_piece,)), dma((n_piece,)), dma((n_piece,)),
            dma((2,)), dma((2,)), dma((4,)), dma((4,)),
            dma((n_l,)), dma((n_l,)), dma((2,)), dma((2,)),
        ],
        compiler_params=pltpu.CompilerParams(
            collective_id=0, has_side_effects=True, vmem_limit_bytes=56 * 1024 * 1024),
        cost_estimate=pl.CostEstimate(flops=8 * 10 ** 9, bytes_accessed=12 * 2 ** 20, transcendentals=0),
    )(rhs, factor, inverses)


def solution(mesh):
    placed = (P(None, "row", "col"), P(None, "row", "col"), P())
    return jax.shard_map(
        functools.partial(shards, mesh.shape["row"]), mesh=mesh, in_specs=placed,
        out_specs=P(None, "row", "col"), check_vma=False)
```

```python
import functools

import jax
import jax.numpy as jnp
from jax import lax
from jax.experimental import pallas as pl
from jax.experimental.pallas import tpu as pltpu
from jax.sharding import PartitionSpec as P

MESH = pl.DeviceIdType.MESH
CW = 256
PR = 32
WINDOW = 10


def split(value):
    high = value.astype(jnp.bfloat16)
    low = (value - high.astype(jnp.float32)).astype(jnp.bfloat16)
    return high, low


def dot3(ah, al, bh, bl):
    def one(a, b):
        return jnp.dot(a, b, preferred_element_type=jnp.float32)

    return one(ah, bh) + one(al, bh) + one(ah, bl)


def kernel(n_row, rhs, fac, inv, out, lane, pan, l10p, invf, mh, ml, ih, il, lh, ll, xh, xl,
           acc_sem, inv_sem, own_sem, zs, zr, ys, yr, xs, xr, ps, pr, ts, tr, ls, lr):
    nb = rhs.shape[1]
    n_chunk = rhs.shape[2] // CW
    ppc = nb // PR
    n_l = ppc // 2
    n_piece = n_chunk * ppc + n_l
    l_at = 2 * ppc
    half = nb // 2

    r = lax.axis_index("row")
    c = lax.axis_index("col")
    z, y = r // 2, r % 2
    n_z = n_row // 2
    core = c % 2
    partner = c + 1 - 2 * core
    peer = (c + 2) % 4
    peer2 = (partner + 2) % 4
    has_up = z < n_z - 1
    has_down = z > 0
    up, down, across = (r + 2, c), (r - 2, c), (r + 1 - 2 * y, c)
    beside, far = (r, partner), (r, peer)

    def load_lead(k):
        cols = pl.ds(k * CW, CW)
        return pltpu.make_async_copy(rhs.at[0, :, cols], out.at[0, :, cols], acc_sem.at[k])

    load_rest = pltpu.make_async_copy(rhs.at[1], out.at[1], acc_sem.at[n_chunk])
    own = [pltpu.make_async_copy(fac.at[j], pan.at[c, j], own_sem.at[j]) for j in range(2)]
    inv_copy = [pltpu.make_async_copy(inv.at[i], invf.at[i], inv_sem.at[i]) for i in range(2)]
    for k in range(n_chunk):
        load_lead(k).start()
    for copy in own + inv_copy + [load_rest]:
        copy.start()

    barrier = pltpu.get_barrier_semaphore()
    for there in (across, beside, far):
        pl.semaphore_signal(barrier, inc=1, device_id=there, device_id_type=MESH)

    @pl.when(has_up)
    def _():
        pl.semaphore_signal(barrier, inc=1, device_id=up, device_id_type=MESH)

    @pl.when(has_down)
    def _():
        pl.semaphore_signal(barrier, inc=1, device_id=down, device_id_type=MESH)

    def fill(k):
        load_lead(k).wait()

        @pl.when(z == 0)
        def _():
            at = k * ppc + (n_l if k >= 2 else 0)
            lane[y, pl.ds(at, ppc)] = out[0, :, k * CW:(k + 1) * CW].reshape(ppc, PR, CW)

    fill(0)
    pl.semaphore_wait(barrier, 3 + has_up.astype(jnp.int32) + has_down.astype(jnp.int32))

    def remote(src, dst, ssem, rsem, there):
        return pltpu.make_async_remote_copy(
            src_ref=src, dst_ref=dst, send_sem=ssem, recv_sem=rsem, device_id=there, device_id_type=MESH)

    def z_copy(p):
        return remote(lane.at[y, p], lane.at[y, p], zs.at[p], zr.at[p], up)

    def y_copy(p):
        return remote(lane.at[y, p], lane.at[y, p], ys.at[p], yr.at[p], across)

    def y_arrival(p):
        return remote(lane.at[1 - y, p], lane.at[1 - y, p], ys.at[p], yr.at[p], across)

    def x_copy(j):
        return remote(fac.at[j], pan.at[c, j], xs.at[j], xr.at[j], far)

    def x_arrival(j):
        return remote(fac.at[j], pan.at[peer, j], xs.at[j], xr.at[j], far)

    def p_copy(i):
        if i < 2:
            return remote(fac.at[i], pan.at[c, i], ps.at[i], pr.at[i], beside)
        return remote(pan.at[peer, i - 2], pan.at[peer, i - 2], ps.at[i], pr.at[i], beside)

    def p_arrival(i):
        at = partner if i < 2 else peer2
        return remote(pan.at[at, i % 2], pan.at[at, i % 2], ps.at[i], pr.at[i], beside)

    def t_copy(i):
        return remote(pan.at[core, 0, pl.ds(i * PR, PR)], lane.at[0, l_at + i], ts.at[i], tr.at[i], across)

    def l_copy(b):
        return remote(lane.at[b, pl.ds(l_at, n_l)], l10p.at[b], ls.at[b], lr.at[b], beside)

    def relay(p):
        @pl.when(has_down)
        def _():
            z_copy(p).wait_recv()

        @pl.when(jnp.logical_and(z == 0, p >= WINDOW))
        def _():
            y_copy(p - WINDOW).wait_send()

            @pl.when(has_up)
            def _():
                z_copy(p - WINDOW).wait_send()

        @pl.when(has_up)
        def _():
            z_copy(p).start()

        y_copy(p).start()

    def relays(start, stop):
        @pl.loop(start, stop)
        def _(p):
            relay(p)

    x_copy(0).start()
    p_copy(0).start()
    p_copy(1).start()
    relays(0, 4)
    for k in range(1, n_chunk):
        fill(k)
        relay(3 + k)

    @pl.when(r < 2)
    def _():
        out[0] = jnp.zeros_like(out[0])

    relays(7, 9)
    for i in range(2):
        inv_copy[i].wait()
        for h in range(2):
            rows = slice(h * half, (h + 1) * half)
            ih[i, rows], il[i, rows] = split(invf[i, rows])
            relay(9 + 2 * i + h)
    relays(13, 18)

    x_arrival(0).wait_recv()
    p_copy(2).start()
    x_copy(1).start()
    for copy in own:
        copy.wait()

    @pl.when(r == 1)
    def _():
        for i in range(n_l):
            t_copy(i).start()
        lane[1, pl.ds(l_at, n_l)] = pan[core, 0, pl.ds(half, half)].reshape(n_l, PR, CW)

    relays(18, 25)
    for i in range(3):
        p_arrival(i).wait_recv()

    at_row = lax.broadcasted_iota(jnp.int32, (half, CW), 0)
    at_col = lax.broadcasted_iota(jnp.int32, (half, CW), 1)
    minus_one = jnp.where(at_row == at_col, -1.0, 0.0).astype(jnp.float32)

    def panel(q, t):
        j, m = t // 2, t % 2
        value = pan[q, j, m * half:(m + 1) * half]
        if j:
            return value
        mine = minus_one if q % 2 == m else jnp.zeros_like(minus_one)
        solved = jnp.where(r == q // 2, mine, jnp.zeros_like(mine))
        return jnp.where(r < 2, solved, value)

    def triangle(i, parts):
        (ah, al), (bh, bl) = parts
        first = (dot3(ah, al, ih[i, :half, :half], il[i, :half, :half])
                 + dot3(bh, bl, ih[i, half:, :half], il[i, half:, :half]))
        return first, dot3(bh, bl, ih[i, half:, half:], il[i, half:, half:])

    def keep(t, b, products):
        rows = slice(t * half, (t + 1) * half)
        for h, value in enumerate(products):
            at = slice((2 * h + b) * CW, (2 * h + b + 1) * CW)
            mh[rows, at], ml[rows, at] = split(value)

    def second_factor(t):
        keep(t, 1, triangle(1, [split(panel(2, t)), split(panel(3, t))]))

    def first_factor(t):
        rows = slice(t * half, (t + 1) * half)
        parts = []
        for q in range(2):
            value = panel(q, t)
            for h in range(2):
                at = slice((2 * h + 1) * CW, (2 * h + 2) * CW)
                ks = slice(h * half, (h + 1) * half)
                value = value - dot3(mh[rows, at], ml[rows, at], lh[q, ks], ll[q, ks])
            parts.append(split(value))
        keep(t, 0, triangle(0, parts))

    second_factor(0)
    relays(25, 27)
    second_factor(1)
    relays(27, 32)

    @pl.when(r == 0)
    def _():
        for i in range(n_l):
            t_copy(i).wait_recv()

    relays(32, 38)
    x_arrival(1).wait_recv()
    p_copy(3).start()
    relays(38, 42)
    for i in range(n_l):
        y_arrival(l_at + i).wait_recv()
    for b in range(2):
        l_copy(b).start()
    relay(42)
    p_arrival(3).wait_recv()
    second_factor(2)
    relay(43)
    second_factor(3)
    relay(44)
    for b in range(2):
        l_copy(b).wait_recv()
        for at, block in ((core, lane[b, pl.ds(l_at, n_l)]), (1 - core, l10p[b])):
            h, l = split(block.reshape(half, CW))
            lh[at, pl.ds(b * half, half)] = h
            ll[at, pl.ds(b * half, half)] = l
    load_rest.wait()
    for t in range(4):
        relay(45 + 2 * t)
        first_factor(t)
        relay(46 + 2 * t)

    def gather(g):
        k, h = g // 2, g % 2
        start = k * ppc + jnp.where(k >= 2, n_l, 0) + h * n_l

        @pl.loop(start, start + n_l)
        def _(p):
            y_arrival(p).wait_recv()

        for b in range(2):
            rows = slice(b * half, (b + 1) * half)
            xh[rows], xl[rows] = split(lane[b, pl.ds(start, n_l)].reshape(half, CW))

    def update(g, t):
        k, h = g // 2, g % 2
        rows = pl.ds(pl.multiple_of(t * half, half), half)
        place = (t // 2, pl.ds(pl.multiple_of((t % 2) * half, half), half), pl.ds(pl.multiple_of(k * CW, CW), CW))
        ks = pl.ds(pl.multiple_of(h * 2 * CW, 2 * CW), 2 * CW)
        out[place] = out[place] - dot3(mh[rows, ks], ml[rows, ks], xh[...], xl[...])

    @pl.loop(0, 4 * 2 * n_chunk)
    def _(n):
        g, t = n // 4, n % 4

        @pl.when(jnp.logical_and(g < 6, t < 3))
        def _():
            relay(53 + 3 * g + t)

        @pl.when(n == 24)
        def _():
            relays(71, n_piece)

        @pl.when(t == 0)
        def _():
            gather(g)

        update(g, t)

    x_copy(0).wait_send()
    x_copy(1).wait_send()
    for i in range(4):
        p_copy(i).wait_send()
    for b in range(2):
        l_copy(b).wait_send()

    @pl.when(r == 1)
    def _():
        for i in range(n_l):
            t_copy(i).wait_send()

    @pl.loop(jnp.where(z == 0, n_piece - WINDOW, 0), n_piece)
    def _(p):
        y_copy(p).wait_send()

        @pl.when(has_up)
        def _():
            z_copy(p).wait_send()


def shards(n_row, rhs, factor, inverses):
    nb = rhs.shape[1]
    n_chunk = rhs.shape[2] // CW
    ppc = nb // PR
    n_l = ppc // 2
    n_piece = n_chunk * ppc + n_l
    f32, bf16, dma = jnp.float32, jnp.bfloat16, pltpu.SemaphoreType.DMA
    anywhere = pl.BlockSpec(memory_space=pl.ANY)
    return pl.pallas_call(
        functools.partial(kernel, n_row),
        out_shape=pltpu.VMEM(rhs.shape, f32),
        in_specs=[anywhere] * 3,
        out_specs=pl.BlockSpec(memory_space=pltpu.VMEM),
        scratch_shapes=[
            pltpu.VMEM((2, n_piece, PR, CW), f32),
            pltpu.VMEM((4, 2, nb, CW), f32),
            pltpu.VMEM((2, n_l, PR, CW), f32),
            pltpu.VMEM((2, nb, nb), f32),
            pltpu.VMEM((2 * nb, 2 * nb), bf16),
            pltpu.VMEM((2 * nb, 2 * nb), bf16),
            pltpu.VMEM((2, nb, nb), bf16),
            pltpu.VMEM((2, nb, nb), bf16),
            pltpu.VMEM((2, nb, CW), bf16),
            pltpu.VMEM((2, nb, CW), bf16),
            pltpu.VMEM((nb, CW), bf16),
            pltpu.VMEM((nb, CW), bf16),
            dma((n_chunk + 1,)), dma((2,)), dma((2,)),
            dma((n_piece,)), dma((n_piece,)), dma((n_piece,)), dma((n_piece,)),
            dma((2,)), dma((2,)), dma((4,)), dma((4,)),
            dma((n_l,)), dma((n_l,)), dma((2,)), dma((2,)),
        ],
        compiler_params=pltpu.CompilerParams(
            collective_id=0, has_side_effects=True, vmem_limit_bytes=59 * 1024 * 1024),
        cost_estimate=pl.CostEstimate(flops=8 * 10 ** 9, bytes_accessed=12 * 2 ** 20, transcendentals=0),
    )(rhs, factor, inverses)


def solution(mesh):
    placed = (P(None, "row", "col"), P(None, "row", "col"), P())
    return jax.shard_map(
        functools.partial(shards, mesh.shape["row"]), mesh=mesh, in_specs=placed,
        out_specs=P(None, "row", "col"), check_vma=False)
```

```python
import functools

import jax
import jax.numpy as jnp
from jax import lax
from jax.experimental import pallas as pl
from jax.experimental.pallas import tpu as pltpu
from jax.sharding import PartitionSpec as P

MESH = pl.DeviceIdType.MESH
CW = 256
PR = 32
WINDOW = 10


def split(value):
    high = value.astype(jnp.bfloat16)
    low = (value - high.astype(jnp.float32)).astype(jnp.bfloat16)
    return high, low


def dot3(ah, al, bh, bl):
    def one(a, b):
        return jnp.dot(a, b, preferred_element_type=jnp.float32)

    return one(ah, bh) + one(al, bh) + one(ah, bl)


def kernel(n_row, rhs, fac, inv, out, lane, pan, l10p, invf, mh, ml, ih, il, lh, ll, xh, xl,
           acc_sem, inv_sem, own_sem, zs, zr, ys, yr, xs, xr, ps, pr, ts, tr, ls, lr):
    nb = rhs.shape[1]
    n_chunk = rhs.shape[2] // CW
    ppc = nb // PR
    n_l = ppc // 2
    n_piece = n_chunk * ppc + n_l
    l_at = 2 * ppc
    half = nb // 2

    r = lax.axis_index("row")
    c = lax.axis_index("col")
    z, y = r // 2, r % 2
    n_z = n_row // 2
    core = c % 2
    partner = c + 1 - 2 * core
    peer = (c + 2) % 4
    peer2 = (partner + 2) % 4
    has_up = z < n_z - 1
    has_down = z > 0
    up, down, across = (r + 2, c), (r - 2, c), (r + 1 - 2 * y, c)
    beside, far = (r, partner), (r, peer)

    def load_lead(k):
        cols = pl.ds(k * CW, CW)
        return pltpu.make_async_copy(rhs.at[0, :, cols], out.at[0, :, cols], acc_sem.at[k])

    load_rest = pltpu.make_async_copy(rhs.at[1], out.at[1], acc_sem.at[n_chunk])
    own = [pltpu.make_async_copy(fac.at[j], pan.at[c, j], own_sem.at[j]) for j in range(2)]
    inv_copy = [pltpu.make_async_copy(inv.at[i], invf.at[i], inv_sem.at[i]) for i in range(2)]
    for k in range(n_chunk):
        load_lead(k).start()
    for copy in own + inv_copy + [load_rest]:
        copy.start()

    barrier = pltpu.get_barrier_semaphore()
    for there in (across, beside, far):
        pl.semaphore_signal(barrier, inc=1, device_id=there, device_id_type=MESH)

    @pl.when(has_up)
    def _():
        pl.semaphore_signal(barrier, inc=1, device_id=up, device_id_type=MESH)

    @pl.when(has_down)
    def _():
        pl.semaphore_signal(barrier, inc=1, device_id=down, device_id_type=MESH)

    def fill(k):
        load_lead(k).wait()

        @pl.when(z == 0)
        def _():
            at = k * ppc + (n_l if k >= 2 else 0)
            lane[y, pl.ds(at, ppc)] = out[0, :, k * CW:(k + 1) * CW].reshape(ppc, PR, CW)

    fill(0)
    pl.semaphore_wait(barrier, 3 + has_up.astype(jnp.int32) + has_down.astype(jnp.int32))

    def remote(src, dst, ssem, rsem, there):
        return pltpu.make_async_remote_copy(
            src_ref=src, dst_ref=dst, send_sem=ssem, recv_sem=rsem, device_id=there, device_id_type=MESH)

    def z_copy(p):
        return remote(lane.at[y, p], lane.at[y, p], zs.at[p], zr.at[p], up)

    def y_copy(p):
        return remote(lane.at[y, p], lane.at[y, p], ys.at[p], yr.at[p], across)

    def y_arrival(p):
        return remote(lane.at[1 - y, p], lane.at[1 - y, p], ys.at[p], yr.at[p], across)

    def x_copy(j):
        return remote(fac.at[j], pan.at[c, j], xs.at[j], xr.at[j], far)

    def x_arrival(j):
        return remote(fac.at[j], pan.at[peer, j], xs.at[j], xr.at[j], far)

    def p_copy(i):
        if i < 2:
            return remote(fac.at[i], pan.at[c, i], ps.at[i], pr.at[i], beside)
        return remote(pan.at[peer, i - 2], pan.at[peer, i - 2], ps.at[i], pr.at[i], beside)

    def p_arrival(i):
        at = partner if i < 2 else peer2
        return remote(pan.at[at, i % 2], pan.at[at, i % 2], ps.at[i], pr.at[i], beside)

    def t_copy(i):
        return remote(pan.at[core, 0, pl.ds(i * PR, PR)], lane.at[0, l_at + i], ts.at[i], tr.at[i], across)

    def l_copy(b):
        return remote(lane.at[b, pl.ds(l_at, n_l)], l10p.at[b], ls.at[b], lr.at[b], beside)

    def relay(p):
        @pl.when(has_down)
        def _():
            z_copy(p).wait_recv()

        @pl.when(jnp.logical_and(z == 0, p >= WINDOW))
        def _():
            y_copy(p - WINDOW).wait_send()

            @pl.when(has_up)
            def _():
                z_copy(p - WINDOW).wait_send()

        @pl.when(has_up)
        def _():
            z_copy(p).start()

        y_copy(p).start()

    def relays(start, stop):
        @pl.loop(start, stop)
        def _(p):
            relay(p)

    x_copy(0).start()
    p_copy(0).start()
    p_copy(1).start()
    relays(0, 4)
    for k in range(1, n_chunk):
        fill(k)
        relay(3 + k)

    @pl.when(r < 2)
    def _():
        out[0] = jnp.zeros_like(out[0])

    relays(7, 9)
    for i in range(2):
        inv_copy[i].wait()
        for h in range(2):
            rows = slice(h * half, (h + 1) * half)
            ih[i, rows], il[i, rows] = split(invf[i, rows])
            relay(9 + 2 * i + h)
    x_copy(1).start()
    relays(13, 18)

    x_arrival(0).wait_recv()
    p_copy(2).start()
    for copy in own:
        copy.wait()

    @pl.when(r == 1)
    def _():
        for i in range(n_l):
            t_copy(i).start()
        lane[1, pl.ds(l_at, n_l)] = pan[core, 0, pl.ds(half, half)].reshape(n_l, PR, CW)

    relays(18, 25)
    for i in range(3):
        p_arrival(i).wait_recv()

    at_row = lax.broadcasted_iota(jnp.int32, (half, CW), 0)
    at_col = lax.broadcasted_iota(jnp.int32, (half, CW), 1)
    minus_one = jnp.where(at_row == at_col, -1.0, 0.0).astype(jnp.float32)

    def panel(q, t):
        j, m = t // 2, t % 2
        value = pan[q, j, m * half:(m + 1) * half]
        if j:
            return value
        mine = minus_one if q % 2 == m else jnp.zeros_like(minus_one)
        solved = jnp.where(r == q // 2, mine, jnp.zeros_like(mine))
        return jnp.where(r < 2, solved, value)

    def triangle(i, parts):
        (ah, al), (bh, bl) = parts
        first = (dot3(ah, al, ih[i, :half, :half], il[i, :half, :half])
                 + dot3(bh, bl, ih[i, half:, :half], il[i, half:, :half]))
        return first, dot3(bh, bl, ih[i, half:, half:], il[i, half:, half:])

    def keep(t, b, products):
        rows = slice(t * half, (t + 1) * half)
        for h, value in enumerate(products):
            at = slice((2 * h + b) * CW, (2 * h + b + 1) * CW)
            mh[rows, at], ml[rows, at] = split(value)

    def second_factor(t):
        keep(t, 1, triangle(1, [split(panel(2, t)), split(panel(3, t))]))

    def first_factor(t):
        rows = slice(t * half, (t + 1) * half)
        parts = []
        for q in range(2):
            value = panel(q, t)
            for h in range(2):
                at = slice((2 * h + 1) * CW, (2 * h + 2) * CW)
                ks = slice(h * half, (h + 1) * half)
                value = value - dot3(mh[rows, at], ml[rows, at], lh[q, ks], ll[q, ks])
            parts.append(split(value))
        keep(t, 0, triangle(0, parts))

    second_factor(0)
    relays(25, 27)
    second_factor(1)
    relays(27, 32)

    @pl.when(r == 0)
    def _():
        for i in range(n_l):
            t_copy(i).wait_recv()

    relays(32, 41)
    x_arrival(1).wait_recv()
    p_copy(3).start()
    relays(41, 43)
    for i in range(n_l):
        y_arrival(l_at + i).wait_recv()
    for b in range(2):
        l_copy(b).start()
    relays(43, 45)
    p_arrival(3).wait_recv()
    second_factor(2)
    relay(45)
    second_factor(3)
    relays(46, 49)
    for b in range(2):
        l_copy(b).wait_recv()
        for at, block in ((core, lane[b, pl.ds(l_at, n_l)]), (1 - core, l10p[b])):
            h, l = split(block.reshape(half, CW))
            lh[at, pl.ds(b * half, half)] = h
            ll[at, pl.ds(b * half, half)] = l
    load_rest.wait()
    for t in range(4):
        relay(49 + t)
        first_factor(t)

    def gather(g):
        k, h = g // 2, g % 2
        start = k * ppc + jnp.where(k >= 2, n_l, 0) + h * n_l

        @pl.loop(start, start + n_l)
        def _(p):
            y_arrival(p).wait_recv()

        for b in range(2):
            rows = slice(b * half, (b + 1) * half)
            xh[rows], xl[rows] = split(lane[b, pl.ds(start, n_l)].reshape(half, CW))

    def update(g, t):
        k, h = g // 2, g % 2
        rows = pl.ds(pl.multiple_of(t * half, half), half)
        place = (t // 2, pl.ds(pl.multiple_of((t % 2) * half, half), half), pl.ds(pl.multiple_of(k * CW, CW), CW))
        ks = pl.ds(pl.multiple_of(h * 2 * CW, 2 * CW), 2 * CW)
        out[place] = out[place] - dot3(mh[rows, ks], ml[rows, ks], xh[...], xl[...])

    @pl.loop(0, 4 * 2 * n_chunk)
    def _(n):
        g, t = n // 4, n % 4

        @pl.when(jnp.logical_and(g < 6, t < 3))
        def _():
            relay(53 + 3 * g + t)

        @pl.when(n == 24)
        def _():
            relays(71, n_piece)

        @pl.when(t == 0)
        def _():
            gather(g)

        update(g, t)

    x_copy(0).wait_send()
    x_copy(1).wait_send()
    for i in range(4):
        p_copy(i).wait_send()
    for b in range(2):
        l_copy(b).wait_send()

    @pl.when(r == 1)
    def _():
        for i in range(n_l):
            t_copy(i).wait_send()

    @pl.loop(jnp.where(z == 0, n_piece - WINDOW, 0), n_piece)
    def _(p):
        y_copy(p).wait_send()

        @pl.when(has_up)
        def _():
            z_copy(p).wait_send()


def shards(n_row, rhs, factor, inverses):
    nb = rhs.shape[1]
    n_chunk = rhs.shape[2] // CW
    ppc = nb // PR
    n_l = ppc // 2
    n_piece = n_chunk * ppc + n_l
    f32, bf16, dma = jnp.float32, jnp.bfloat16, pltpu.SemaphoreType.DMA
    anywhere = pl.BlockSpec(memory_space=pl.ANY)
    return pl.pallas_call(
        functools.partial(kernel, n_row),
        out_shape=pltpu.VMEM(rhs.shape, f32),
        in_specs=[anywhere] * 3,
        out_specs=pl.BlockSpec(memory_space=pltpu.VMEM),
        scratch_shapes=[
            pltpu.VMEM((2, n_piece, PR, CW), f32),
            pltpu.VMEM((4, 2, nb, CW), f32),
            pltpu.VMEM((2, n_l, PR, CW), f32),
            pltpu.VMEM((2, nb, nb), f32),
            pltpu.VMEM((2 * nb, 2 * nb), bf16),
            pltpu.VMEM((2 * nb, 2 * nb), bf16),
            pltpu.VMEM((2, nb, nb), bf16),
            pltpu.VMEM((2, nb, nb), bf16),
            pltpu.VMEM((2, nb, CW), bf16),
            pltpu.VMEM((2, nb, CW), bf16),
            pltpu.VMEM((nb, CW), bf16),
            pltpu.VMEM((nb, CW), bf16),
            dma((n_chunk + 1,)), dma((2,)), dma((2,)),
            dma((n_piece,)), dma((n_piece,)), dma((n_piece,)), dma((n_piece,)),
            dma((2,)), dma((2,)), dma((4,)), dma((4,)),
            dma((n_l,)), dma((n_l,)), dma((2,)), dma((2,)),
        ],
        compiler_params=pltpu.CompilerParams(
            collective_id=0, has_side_effects=True, vmem_limit_bytes=59 * 1024 * 1024),
        cost_estimate=pl.CostEstimate(flops=8 * 10 ** 9, bytes_accessed=12 * 2 ** 20, transcendentals=0),
    )(rhs, factor, inverses)


def solution(mesh):
    placed = (P(None, "row", "col"), P(None, "row", "col"), P())
    return jax.shard_map(
        functools.partial(shards, mesh.shape["row"]), mesh=mesh, in_specs=placed,
        out_specs=P(None, "row", "col"), check_vma=False)
```

```python
import functools

import jax
import jax.numpy as jnp
from jax import lax
from jax.experimental import pallas as pl
from jax.experimental.pallas import tpu as pltpu
from jax.sharding import PartitionSpec as P

MESH = pl.DeviceIdType.MESH
CW = 256
PR = 32
Z_WINDOW = 16
Y_WINDOW = 28


def split(value):
    high = value.astype(jnp.bfloat16)
    low = (value - high.astype(jnp.float32)).astype(jnp.bfloat16)
    return high, low


def dot3(ah, al, bh, bl):
    def one(a, b):
        return jnp.dot(a, b, preferred_element_type=jnp.float32)

    return one(ah, bh) + one(al, bh) + one(ah, bl)


def kernel(n_row, rhs, fac, inv, out, lane, pan, l10p, l10x, invf, mh, ml, ih, il, lh, ll, xh, xl,
           acc_sem, inv_sem, own_sem, zs, zr, ys, yr, xs, xr, ps, pr, ts, tr, ls, lr, us, ur):
    nb = rhs.shape[1]
    n_chunk = rhs.shape[2] // CW
    ppc = nb // PR
    n_h = ppc // 2
    n_l = ppc // 4
    n_piece = n_chunk * ppc + n_l
    l_at = 3 * n_h
    half, quarter = nb // 2, nb // 4

    r = lax.axis_index("row")
    c = lax.axis_index("col")
    z, y = r // 2, r % 2
    n_z = n_row // 2
    core, x = c % 2, c // 2
    partner = c + 1 - 2 * core
    peer = (c + 2) % 4
    peer2 = (partner + 2) % 4
    has_up = z < n_z - 1
    has_down = z > 0
    up, down, across = (r + 2, c), (r - 2, c), (r + 1 - 2 * y, c)
    beside, far = (r, partner), (r, peer)

    def load_lead(k):
        cols = pl.ds(k * CW, CW)
        return pltpu.make_async_copy(rhs.at[0, :, cols], out.at[0, :, cols], acc_sem.at[k])

    load_rest = pltpu.make_async_copy(rhs.at[1], out.at[1], acc_sem.at[n_chunk])
    own = [pltpu.make_async_copy(fac.at[j], pan.at[c, j], own_sem.at[j]) for j in range(2)]
    inv_copy = [pltpu.make_async_copy(inv.at[i], invf.at[i], inv_sem.at[i]) for i in range(2)]
    for k in range(n_chunk):
        load_lead(k).start()
    for copy in own + inv_copy + [load_rest]:
        copy.start()

    barrier = pltpu.get_barrier_semaphore()
    for there in (across, beside, far):
        pl.semaphore_signal(barrier, inc=1, device_id=there, device_id_type=MESH)

    @pl.when(has_up)
    def _():
        pl.semaphore_signal(barrier, inc=1, device_id=up, device_id_type=MESH)

    @pl.when(has_down)
    def _():
        pl.semaphore_signal(barrier, inc=1, device_id=down, device_id_type=MESH)

    def first_piece(g):
        return g * n_h + (n_l if g >= 3 else 0)

    def fill(k):
        load_lead(k).wait()

        @pl.when(z == 0)
        def _():
            for h in range(2):
                block = out[0, h * half:(h + 1) * half, k * CW:(k + 1) * CW]
                lane[y, pl.ds(first_piece(2 * k + h), n_h)] = block.reshape(n_h, PR, CW)

    fill(0)
    pl.semaphore_wait(barrier, 3 + has_up.astype(jnp.int32) + has_down.astype(jnp.int32))

    def remote(src, dst, ssem, rsem, there):
        return pltpu.make_async_remote_copy(
            src_ref=src, dst_ref=dst, send_sem=ssem, recv_sem=rsem, device_id=there, device_id_type=MESH)

    def z_copy(p):
        return remote(lane.at[y, p], lane.at[y, p], zs.at[p], zr.at[p], up)

    def y_copy(p):
        return remote(lane.at[y, p], lane.at[y, p], ys.at[p], yr.at[p], across)

    def y_arrival(p):
        return remote(lane.at[1 - y, p], lane.at[1 - y, p], ys.at[p], yr.at[p], across)

    def x_ref(ref, at, i):
        part = ref.at[0] if i < 4 else ref.at[1]
        if at is not None:
            part = ref.at[at, 0] if i < 4 else ref.at[at, 1]
        return part.at[pl.ds((1, 3, 0, 2)[i] * quarter, quarter)] if i < 4 else part

    def x_copy(i):
        return remote(x_ref(fac, None, i), x_ref(pan, c, i), xs.at[i], xr.at[i], far)

    def x_arrival(i):
        return remote(x_ref(fac, None, i), x_ref(pan, peer, i), xs.at[i], xr.at[i], far)

    def p_copy(i):
        if i < 2:
            return remote(fac.at[i], pan.at[c, i], ps.at[i], pr.at[i], beside)
        return remote(pan.at[peer, i - 2], pan.at[peer, i - 2], ps.at[i], pr.at[i], beside)

    def p_arrival(i):
        at = partner if i < 2 else peer2
        return remote(pan.at[at, i % 2], pan.at[at, i % 2], ps.at[i], pr.at[i], beside)

    def t_copy(i):
        rows = pl.ds(pl.multiple_of(x * quarter + i * PR, PR), PR)
        return remote(pan.at[core, 0, rows], lane.at[0, l_at + i], ts.at[i], tr.at[i], across)

    def lx_copy(b):
        return remote(lane.at[b, pl.ds(l_at, n_l)], l10x.at[b], us.at[b], ur.at[b], far)

    def lp_copy(i, b):
        src = l10x.at[b] if i else lane.at[b, pl.ds(l_at, n_l)]
        return remote(src, l10p.at[i, b], ls.at[i, b], lr.at[i, b], beside)

    def relay(p):
        @pl.when(has_down)
        def _():
            z_copy(p).wait_recv()

        @pl.when(jnp.logical_and(jnp.logical_and(z == 0, has_up), p >= Z_WINDOW))
        def _():
            z_copy(p - Z_WINDOW).wait_send()

        @pl.when(has_up)
        def _():
            z_copy(p).start()

        @pl.when(jnp.logical_and(z == 0, p >= Y_WINDOW))
        def _():
            y_copy(p - Y_WINDOW).wait_send()

        y_copy(p).start()

    def relays(start, stop):
        @pl.loop(start, stop)
        def _(p):
            relay(p)

    x_copy(0).start()
    x_copy(1).start()
    p_copy(0).start()
    p_copy(1).start()
    relays(0, 4)
    for k in range(1, n_chunk):
        fill(k)
        relay(3 + k)

    @pl.when(r < 2)
    def _():
        out[0] = jnp.zeros_like(out[0])

    relay(7)
    x_copy(2).start()
    x_copy(3).start()
    for i in range(2):
        inv_copy[i].wait()
        for h in range(2):
            rows = slice(h * half, (h + 1) * half)
            ih[i, rows], il[i, rows] = split(invf[i, rows])
            relay(8 + 2 * i + h)
        if i == 0:
            x_arrival(0).wait_recv()
            x_arrival(1).wait_recv()
            for copy in own:
                copy.wait()

            @pl.when(r == 1)
            def _():
                for e in range(n_l):
                    t_copy(e).start()
                rows = pl.ds(pl.multiple_of(half + x * quarter, quarter), quarter)
                lane[1, pl.ds(l_at, n_l)] = pan[core, 0, rows].reshape(n_l, PR, CW)

    relays(12, 16)
    x_copy(4).start()
    relays(16, 19)
    x_arrival(2).wait_recv()
    x_arrival(3).wait_recv()
    p_copy(2).start()
    relays(19, 24)

    @pl.when(r == 0)
    def _():
        for i in range(n_l):
            t_copy(i).wait_recv()

    relays(24, 26)
    for i in range(3):
        p_arrival(i).wait_recv()

    at_row = lax.broadcasted_iota(jnp.int32, (half, CW), 0)
    at_col = lax.broadcasted_iota(jnp.int32, (half, CW), 1)
    minus_one = jnp.where(at_row == at_col, -1.0, 0.0).astype(jnp.float32)

    def panel(q, t):
        j, m = t // 2, t % 2
        value = pan[q, j, m * half:(m + 1) * half]
        if j:
            return value
        mine = minus_one if q % 2 == m else jnp.zeros_like(minus_one)
        solved = jnp.where(r == q // 2, mine, jnp.zeros_like(mine))
        return jnp.where(r < 2, solved, value)

    def triangle(i, parts):
        (ah, al), (bh, bl) = parts
        first = (dot3(ah, al, ih[i, :half, :half], il[i, :half, :half])
                 + dot3(bh, bl, ih[i, half:, :half], il[i, half:, :half]))
        return first, dot3(bh, bl, ih[i, half:, half:], il[i, half:, half:])

    def keep(t, b, products):
        rows = slice(t * half, (t + 1) * half)
        for h, value in enumerate(products):
            at = slice((2 * h + b) * CW, (2 * h + b + 1) * CW)
            mh[rows, at], ml[rows, at] = split(value)

    def second_factor(t):
        keep(t, 1, triangle(1, [split(panel(2, t)), split(panel(3, t))]))

    def first_factor(t):
        rows = slice(t * half, (t + 1) * half)
        parts = []
        for q in range(2):
            value = panel(q, t)
            for h in range(2):
                at = slice((2 * h + 1) * CW, (2 * h + 2) * CW)
                ks = slice(h * half, (h + 1) * half)
                value = value - dot3(mh[rows, at], ml[rows, at], lh[q, ks], ll[q, ks])
            parts.append(split(value))
        keep(t, 0, triangle(0, parts))

    second_factor(0)
    relay(26)
    second_factor(1)
    relays(27, 32)
    for i in range(n_l):
        y_arrival(l_at + i).wait_recv()
    for b in range(2):
        lp_copy(0, b).start()
        lx_copy(b).start()
    relays(32, 38)
    x_arrival(4).wait_recv()
    p_copy(3).start()
    relays(38, 42)
    for b in range(2):
        lx_copy(b).wait_recv()
        lp_copy(1, b).start()
    relay(42)
    p_arrival(3).wait_recv()
    second_factor(2)
    relay(43)
    second_factor(3)
    relays(44, 46)
    for b in range(2):
        lp_copy(0, b).wait_recv()
        lp_copy(1, b).wait_recv()
        for at, e, block in ((core, x, lane[b, pl.ds(l_at, n_l)]), (core, 1 - x, l10x[b]),
                             (1 - core, x, l10p[0, b]), (1 - core, 1 - x, l10p[1, b])):
            h, l = split(block.reshape(quarter, CW))
            rows = pl.ds(pl.multiple_of(b * half + e * quarter, quarter), quarter)
            lh[at, rows] = h
            ll[at, rows] = l
    load_rest.wait()
    for t in range(4):
        relay(46 + t)
        first_factor(t)

    def gather(g):
        start = g * n_h + jnp.where(g >= 3, n_l, 0)

        @pl.loop(start, start + n_h)
        def _(p):
            y_arrival(p).wait_recv()

        for b in range(2):
            rows = slice(b * half, (b + 1) * half)
            xh[rows], xl[rows] = split(lane[b, pl.ds(start, n_h)].reshape(half, CW))

    def update(g, t):
        k, h = g // 2, g % 2
        rows = pl.ds(pl.multiple_of(t * half, half), half)
        place = (t // 2, pl.ds(pl.multiple_of((t % 2) * half, half), half), pl.ds(pl.multiple_of(k * CW, CW), CW))
        ks = pl.ds(pl.multiple_of(h * 2 * CW, 2 * CW), 2 * CW)
        out[place] = out[place] - dot3(mh[rows, ks], ml[rows, ks], xh[...], xl[...])

    @pl.loop(0, 4 * 2 * n_chunk)
    def _(n):
        g, t = n // 4, n % 4

        @pl.when(jnp.logical_and(g < 6, t < 3))
        def _():
            relay(50 + 3 * g + t)

        @pl.when(t == 0)
        def _():
            gather(g)

        update(g, t)

    for i in range(5):
        x_copy(i).wait_send()
    for i in range(4):
        p_copy(i).wait_send()
    for b in range(2):
        lx_copy(b).wait_send()
        lp_copy(0, b).wait_send()
        lp_copy(1, b).wait_send()

    @pl.when(r == 1)
    def _():
        for i in range(n_l):
            t_copy(i).wait_send()

    @pl.loop(jnp.where(z == 0, n_piece - Y_WINDOW, 0), n_piece)
    def _(p):
        y_copy(p).wait_send()

    @pl.when(has_up)
    def _():
        @pl.loop(jnp.where(z == 0, n_piece - Z_WINDOW, 0), n_piece)
        def _(p):
            z_copy(p).wait_send()


def shards(n_row, rhs, factor, inverses):
    nb = rhs.shape[1]
    n_chunk = rhs.shape[2] // CW
    ppc = nb // PR
    n_l = ppc // 4
    n_piece = n_chunk * ppc + n_l
    f32, bf16, dma = jnp.float32, jnp.bfloat16, pltpu.SemaphoreType.DMA
    anywhere = pl.BlockSpec(memory_space=pl.ANY)
    return pl.pallas_call(
        functools.partial(kernel, n_row),
        out_shape=pltpu.VMEM(rhs.shape, f32),
        in_specs=[anywhere] * 3,
        out_specs=pl.BlockSpec(memory_space=pltpu.VMEM),
        scratch_shapes=[
            pltpu.VMEM((2, n_piece, PR, CW), f32),
            pltpu.VMEM((4, 2, nb, CW), f32),
            pltpu.VMEM((2, 2, n_l, PR, CW), f32),
            pltpu.VMEM((2, n_l, PR, CW), f32),
            pltpu.VMEM((2, nb, nb), f32),
            pltpu.VMEM((2 * nb, 2 * nb), bf16),
            pltpu.VMEM((2 * nb, 2 * nb), bf16),
            pltpu.VMEM((2, nb, nb), bf16),
            pltpu.VMEM((2, nb, nb), bf16),
            pltpu.VMEM((2, nb, CW), bf16),
            pltpu.VMEM((2, nb, CW), bf16),
            pltpu.VMEM((nb, CW), bf16),
            pltpu.VMEM((nb, CW), bf16),
            dma((n_chunk + 1,)), dma((2,)), dma((2,)),
            dma((n_piece,)), dma((n_piece,)), dma((n_piece,)), dma((n_piece,)),
            dma((5,)), dma((5,)), dma((4,)), dma((4,)),
            dma((n_l,)), dma((n_l,)), dma((2, 2)), dma((2, 2)), dma((2,)), dma((2,)),
        ],
        compiler_params=pltpu.CompilerParams(
            collective_id=0, has_side_effects=True, vmem_limit_bytes=59 * 1024 * 1024),
        cost_estimate=pl.CostEstimate(flops=8 * 10 ** 9, bytes_accessed=12 * 2 ** 20, transcendentals=0),
    )(rhs, factor, inverses)


def solution(mesh):
    placed = (P(None, "row", "col"), P(None, "row", "col"), P())
    return jax.shard_map(
        functools.partial(shards, mesh.shape["row"]), mesh=mesh, in_specs=placed,
        out_specs=P(None, "row", "col"), check_vma=False)
```

```python
import functools

import jax
import jax.numpy as jnp
from jax import lax
from jax.experimental import pallas as pl
from jax.experimental.pallas import tpu as pltpu
from jax.sharding import PartitionSpec as P

MESH = pl.DeviceIdType.MESH
CW = 256
PR = 32
Z_WINDOW = 16
Y_WINDOW = 28


def split(value):
    high = value.astype(jnp.bfloat16)
    low = (value - high.astype(jnp.float32)).astype(jnp.bfloat16)
    return high, low


def dot3(ah, al, bh, bl):
    def one(a, b):
        return jnp.dot(a, b, preferred_element_type=jnp.float32)

    return one(ah, bh) + one(al, bh) + one(ah, bl)


def kernel(n_row, rhs, fac, inv, out, lane, pan, l10p, l10x, invf, mh, ml, ih, il, lh, ll, xh, xl,
           acc_sem, inv_sem, own_sem, zs, zr, ys, yr, xs, xr, ps, pr, ts, tr, ls, lr, us, ur):
    nb = rhs.shape[1]
    n_chunk = rhs.shape[2] // CW
    ppc = nb // PR
    n_h = ppc // 2
    n_l = ppc // 4
    n_piece = n_chunk * ppc + n_l
    l_at = 2 * n_h
    half, quarter = nb // 2, nb // 4

    r = lax.axis_index("row")
    c = lax.axis_index("col")
    z, y = r // 2, r % 2
    n_z = n_row // 2
    core, x = c % 2, c // 2
    partner = c + 1 - 2 * core
    peer = (c + 2) % 4
    peer2 = (partner + 2) % 4
    has_up = z < n_z - 1
    has_down = z > 0
    up, down, across = (r + 2, c), (r - 2, c), (r + 1 - 2 * y, c)
    beside, far = (r, partner), (r, peer)

    def load_lead(k):
        cols = pl.ds(k * CW, CW)
        return pltpu.make_async_copy(rhs.at[0, :, cols], out.at[0, :, cols], acc_sem.at[k])

    load_rest = pltpu.make_async_copy(rhs.at[1], out.at[1], acc_sem.at[n_chunk])
    own = [pltpu.make_async_copy(fac.at[j], pan.at[c, j], own_sem.at[j]) for j in range(2)]
    inv_copy = [pltpu.make_async_copy(inv.at[i], invf.at[i], inv_sem.at[i]) for i in range(2)]
    for k in range(n_chunk):
        load_lead(k).start()
    for copy in own + inv_copy + [load_rest]:
        copy.start()

    barrier = pltpu.get_barrier_semaphore()
    for there in (across, beside, far):
        pl.semaphore_signal(barrier, inc=1, device_id=there, device_id_type=MESH)

    @pl.when(has_up)
    def _():
        pl.semaphore_signal(barrier, inc=1, device_id=up, device_id_type=MESH)

    @pl.when(has_down)
    def _():
        pl.semaphore_signal(barrier, inc=1, device_id=down, device_id_type=MESH)

    def first_piece(g):
        return g * n_h + (n_l if g >= 2 else 0)

    def fill(k):
        load_lead(k).wait()

        @pl.when(z == 0)
        def _():
            for h in range(2):
                block = out[0, h * half:(h + 1) * half, k * CW:(k + 1) * CW]
                lane[y, pl.ds(first_piece(2 * k + h), n_h)] = block.reshape(n_h, PR, CW)

    fill(0)
    pl.semaphore_wait(barrier, 3 + has_up.astype(jnp.int32) + has_down.astype(jnp.int32))

    def remote(src, dst, ssem, rsem, there):
        return pltpu.make_async_remote_copy(
            src_ref=src, dst_ref=dst, send_sem=ssem, recv_sem=rsem, device_id=there, device_id_type=MESH)

    def z_copy(p):
        return remote(lane.at[y, p], lane.at[y, p], zs.at[p], zr.at[p], up)

    def y_copy(p):
        return remote(lane.at[y, p], lane.at[y, p], ys.at[p], yr.at[p], across)

    def y_arrival(p):
        return remote(lane.at[1 - y, p], lane.at[1 - y, p], ys.at[p], yr.at[p], across)

    def x_ref(ref, at, i):
        rows = pl.ds((1, 3, 0, 2)[i] * quarter, quarter) if i < 4 else pl.ds((i - 4) * half, half)
        return ref.at[i // 4, rows] if at is None else ref.at[at, i // 4, rows]

    def x_copy(i):
        return remote(x_ref(fac, None, i), x_ref(pan, c, i), xs.at[i], xr.at[i], far)

    def x_arrival(i):
        return remote(x_ref(fac, None, i), x_ref(pan, peer, i), xs.at[i], xr.at[i], far)

    def p_ref(at, i):
        return pan.at[at, i % 2] if i < 3 else pan.at[at, 1, pl.ds((i - 3) * half, half)]

    def p_copy(i):
        if i < 2:
            return remote(fac.at[i], pan.at[c, i], ps.at[i], pr.at[i], beside)
        return remote(p_ref(peer, i), p_ref(peer, i), ps.at[i], pr.at[i], beside)

    def p_arrival(i):
        at = partner if i < 2 else peer2
        return remote(p_ref(at, i), p_ref(at, i), ps.at[i], pr.at[i], beside)

    def t_copy(i):
        rows = pl.ds(pl.multiple_of(x * quarter + i * PR, PR), PR)
        return remote(pan.at[core, 0, rows], lane.at[0, l_at + i], ts.at[i], tr.at[i], across)

    def lx_copy(b):
        return remote(lane.at[b, pl.ds(l_at, n_l)], l10x.at[b], us.at[b], ur.at[b], far)

    def lp_copy(i, b):
        src = l10x.at[b] if i else lane.at[b, pl.ds(l_at, n_l)]
        return remote(src, l10p.at[i, b], ls.at[i, b], lr.at[i, b], beside)

    def relay(p):
        @pl.when(has_down)
        def _():
            z_copy(p).wait_recv()

        @pl.when(jnp.logical_and(jnp.logical_and(z == 0, has_up), p >= Z_WINDOW))
        def _():
            z_copy(p - Z_WINDOW).wait_send()

        @pl.when(has_up)
        def _():
            z_copy(p).start()

        @pl.when(jnp.logical_and(z == 0, p >= Y_WINDOW))
        def _():
            y_copy(p - Y_WINDOW).wait_send()

        y_copy(p).start()

    def relays(start, stop):
        @pl.loop(start, stop)
        def _(p):
            relay(p)

    x_copy(0).start()
    x_copy(1).start()
    p_copy(0).start()
    p_copy(1).start()
    relays(0, 4)
    for k in range(1, n_chunk):
        fill(k)
        relay(3 + k)

    @pl.when(r < 2)
    def _():
        out[0] = jnp.zeros_like(out[0])

    relay(7)
    x_copy(2).start()
    x_copy(3).start()

    def split_inverse(i, h):
        rows = slice(h * half, (h + 1) * half)
        ih[i, rows], il[i, rows] = split(invf[i, rows])

    inv_copy[0].wait()
    split_inverse(0, 0)
    relay(8)
    x_arrival(0).wait_recv()
    x_arrival(1).wait_recv()
    for copy in own:
        copy.wait()

    @pl.when(r == 1)
    def _():
        for e in range(n_l):
            t_copy(e).start()
        rows = pl.ds(pl.multiple_of(half + x * quarter, quarter), quarter)
        lane[1, pl.ds(l_at, n_l)] = pan[core, 0, rows].reshape(n_l, PR, CW)

    relay(9)
    split_inverse(0, 1)
    relay(10)
    inv_copy[1].wait()
    split_inverse(1, 0)
    relay(11)
    split_inverse(1, 1)
    relay(12)
    x_copy(4).start()
    relays(13, 16)

    @pl.when(r == 0)
    def _():
        for i in range(n_l):
            t_copy(i).wait_recv()

    relays(16, 19)
    x_arrival(2).wait_recv()
    x_arrival(3).wait_recv()
    p_copy(2).start()
    relays(19, 24)
    for i in range(n_l):
        y_arrival(l_at + i).wait_recv()
    for b in range(2):
        lp_copy(0, b).start()
        lx_copy(b).start()
    relays(24, 26)
    for i in range(3):
        p_arrival(i).wait_recv()

    at_row = lax.broadcasted_iota(jnp.int32, (half, CW), 0)
    at_col = lax.broadcasted_iota(jnp.int32, (half, CW), 1)
    minus_one = jnp.where(at_row == at_col, -1.0, 0.0).astype(jnp.float32)

    def panel(q, t):
        j, m = t // 2, t % 2
        value = pan[q, j, m * half:(m + 1) * half]
        if j:
            return value
        mine = minus_one if q % 2 == m else jnp.zeros_like(minus_one)
        solved = jnp.where(r == q // 2, mine, jnp.zeros_like(mine))
        return jnp.where(r < 2, solved, value)

    def triangle(i, parts):
        (ah, al), (bh, bl) = parts
        first = (dot3(ah, al, ih[i, :half, :half], il[i, :half, :half])
                 + dot3(bh, bl, ih[i, half:, :half], il[i, half:, :half]))
        return first, dot3(bh, bl, ih[i, half:, half:], il[i, half:, half:])

    def keep(t, b, products):
        rows = slice(t * half, (t + 1) * half)
        for h, value in enumerate(products):
            at = slice((2 * h + b) * CW, (2 * h + b + 1) * CW)
            mh[rows, at], ml[rows, at] = split(value)

    def second_factor(t):
        keep(t, 1, triangle(1, [split(panel(2, t)), split(panel(3, t))]))

    def first_factor(t):
        rows = slice(t * half, (t + 1) * half)
        parts = []
        for q in range(2):
            value = panel(q, t)
            for h in range(2):
                at = slice((2 * h + 1) * CW, (2 * h + 2) * CW)
                ks = slice(h * half, (h + 1) * half)
                value = value - dot3(mh[rows, at], ml[rows, at], lh[q, ks], ll[q, ks])
            parts.append(split(value))
        keep(t, 0, triangle(0, parts))

    second_factor(0)
    relay(26)
    second_factor(1)
    relay(27)
    x_arrival(4).wait_recv()
    p_copy(3).start()
    relay(28)
    x_copy(5).start()
    relays(29, 33)
    p_arrival(3).wait_recv()
    second_factor(2)
    relays(33, 36)
    for b in range(2):
        lx_copy(b).wait_recv()
        lp_copy(1, b).start()
    relays(36, 39)
    for b in range(2):
        lp_copy(0, b).wait_recv()
        lp_copy(1, b).wait_recv()
        for at, e, block in ((core, x, lane[b, pl.ds(l_at, n_l)]), (core, 1 - x, l10x[b]),
                             (1 - core, x, l10p[0, b]), (1 - core, 1 - x, l10p[1, b])):
            h, l = split(block.reshape(quarter, CW))
            rows = pl.ds(pl.multiple_of(b * half + e * quarter, quarter), quarter)
            lh[at, rows] = h
            ll[at, rows] = l
    load_rest.wait()
    for t in range(3):
        relay(39 + t)
        first_factor(t)
    relay(42)
    x_arrival(5).wait_recv()
    p_copy(4).start()
    relays(43, 46)
    p_arrival(4).wait_recv()
    second_factor(3)
    relay(46)
    first_factor(3)

    def gather(g):
        start = g * n_h + jnp.where(g >= 2, n_l, 0)

        @pl.loop(start, start + n_h)
        def _(p):
            y_arrival(p).wait_recv()

        for b in range(2):
            rows = slice(b * half, (b + 1) * half)
            xh[rows], xl[rows] = split(lane[b, pl.ds(start, n_h)].reshape(half, CW))

    def update(g, t):
        k, h = g // 2, g % 2
        rows = pl.ds(pl.multiple_of(t * half, half), half)
        place = (t // 2, pl.ds(pl.multiple_of((t % 2) * half, half), half), pl.ds(pl.multiple_of(k * CW, CW), CW))
        ks = pl.ds(pl.multiple_of(h * 2 * CW, 2 * CW), 2 * CW)
        out[place] = out[place] - dot3(mh[rows, ks], ml[rows, ks], xh[...], xl[...])

    @pl.loop(0, 4 * 2 * n_chunk)
    def _(n):
        g, t = n // 4, n % 4

        @pl.when(jnp.logical_and(g < 6, n % 8 < 7))
        def _():
            relay(47 + n - n // 8)

        @pl.when(t == 0)
        def _():
            gather(g)

        update(g, t)

    for i in range(6):
        x_copy(i).wait_send()
    for i in range(5):
        p_copy(i).wait_send()
    for b in range(2):
        lx_copy(b).wait_send()
        lp_copy(0, b).wait_send()
        lp_copy(1, b).wait_send()

    @pl.when(r == 1)
    def _():
        for i in range(n_l):
            t_copy(i).wait_send()

    @pl.loop(jnp.where(z == 0, n_piece - Y_WINDOW, 0), n_piece)
    def _(p):
        y_copy(p).wait_send()

    @pl.when(has_up)
    def _():
        @pl.loop(jnp.where(z == 0, n_piece - Z_WINDOW, 0), n_piece)
        def _(p):
            z_copy(p).wait_send()


def shards(n_row, rhs, factor, inverses):
    nb = rhs.shape[1]
    n_chunk = rhs.shape[2] // CW
    ppc = nb // PR
    n_l = ppc // 4
    n_piece = n_chunk * ppc + n_l
    f32, bf16, dma = jnp.float32, jnp.bfloat16, pltpu.SemaphoreType.DMA
    anywhere = pl.BlockSpec(memory_space=pl.ANY)
    return pl.pallas_call(
        functools.partial(kernel, n_row),
        out_shape=pltpu.VMEM(rhs.shape, f32),
        in_specs=[anywhere] * 3,
        out_specs=pl.BlockSpec(memory_space=pltpu.VMEM),
        scratch_shapes=[
            pltpu.VMEM((2, n_piece, PR, CW), f32),
            pltpu.VMEM((4, 2, nb, CW), f32),
            pltpu.VMEM((2, 2, n_l, PR, CW), f32),
            pltpu.VMEM((2, n_l, PR, CW), f32),
            pltpu.VMEM((2, nb, nb), f32),
            pltpu.VMEM((2 * nb, 2 * nb), bf16),
            pltpu.VMEM((2 * nb, 2 * nb), bf16),
            pltpu.VMEM((2, nb, nb), bf16),
            pltpu.VMEM((2, nb, nb), bf16),
            pltpu.VMEM((2, nb, CW), bf16),
            pltpu.VMEM((2, nb, CW), bf16),
            pltpu.VMEM((nb, CW), bf16),
            pltpu.VMEM((nb, CW), bf16),
            dma((n_chunk + 1,)), dma((2,)), dma((2,)),
            dma((n_piece,)), dma((n_piece,)), dma((n_piece,)), dma((n_piece,)),
            dma((6,)), dma((6,)), dma((5,)), dma((5,)),
            dma((n_l,)), dma((n_l,)), dma((2, 2)), dma((2, 2)), dma((2,)), dma((2,)),
        ],
        compiler_params=pltpu.CompilerParams(
            collective_id=0, has_side_effects=True, vmem_limit_bytes=59 * 1024 * 1024),
        cost_estimate=pl.CostEstimate(flops=8 * 10 ** 9, bytes_accessed=12 * 2 ** 20, transcendentals=0),
    )(rhs, factor, inverses)


def solution(mesh):
    placed = (P(None, "row", "col"), P(None, "row", "col"), P())
    return jax.shard_map(
        functools.partial(shards, mesh.shape["row"]), mesh=mesh, in_specs=placed,
        out_specs=P(None, "row", "col"), check_vma=False)
```

```python
import functools

import jax
import jax.numpy as jnp
from jax import lax
from jax.experimental import pallas as pl
from jax.experimental.pallas import tpu as pltpu
from jax.sharding import PartitionSpec as P

MESH = pl.DeviceIdType.MESH
CW = 256
PR = 32
Z_WINDOW = 16
Y_WINDOW = 28


def split(value):
    high = value.astype(jnp.bfloat16)
    low = (value - high.astype(jnp.float32)).astype(jnp.bfloat16)
    return high, low


def dot3(ah, al, bh, bl):
    def one(a, b):
        return jnp.dot(a, b, preferred_element_type=jnp.float32)

    return one(ah, bh) + one(al, bh) + one(ah, bl)


def kernel(n_row, rhs, fac, inv, out, lane, pan, l10p, l10x, invf, mh, ml, ih, il, lh, ll, xh, xl,
           acc_sem, inv_sem, own_sem, zs, zr, ys, yr, xs, xr, ps, pr, ts, tr, ls, lr, us, ur):
    nb = rhs.shape[1]
    n_chunk = rhs.shape[2] // CW
    ppc = nb // PR
    n_h = ppc // 2
    n_l = ppc // 4
    n_piece = n_chunk * ppc + n_l
    l_at = 2 * n_h
    half, quarter = nb // 2, nb // 4

    r = lax.axis_index("row")
    c = lax.axis_index("col")
    z, y = r // 2, r % 2
    n_z = n_row // 2
    core, x = c % 2, c // 2
    partner = c + 1 - 2 * core
    peer = (c + 2) % 4
    peer2 = (partner + 2) % 4
    has_up = z < n_z - 1
    has_down = z > 0
    up, down, across = (r + 2, c), (r - 2, c), (r + 1 - 2 * y, c)
    beside, far = (r, partner), (r, peer)

    def load_lead(k):
        cols = pl.ds(k * CW, CW)
        return pltpu.make_async_copy(rhs.at[0, :, cols], out.at[0, :, cols], acc_sem.at[k])

    load_rest = pltpu.make_async_copy(rhs.at[1], out.at[1], acc_sem.at[n_chunk])
    own = [pltpu.make_async_copy(fac.at[j], pan.at[c, j], own_sem.at[j]) for j in range(2)]
    inv_copy = [pltpu.make_async_copy(inv.at[i], invf.at[i], inv_sem.at[i]) for i in range(2)]
    for k in range(n_chunk):
        load_lead(k).start()
    for copy in own + inv_copy + [load_rest]:
        copy.start()

    barrier = pltpu.get_barrier_semaphore()
    for there in (across, beside, far):
        pl.semaphore_signal(barrier, inc=1, device_id=there, device_id_type=MESH)

    @pl.when(has_up)
    def _():
        pl.semaphore_signal(barrier, inc=1, device_id=up, device_id_type=MESH)

    @pl.when(has_down)
    def _():
        pl.semaphore_signal(barrier, inc=1, device_id=down, device_id_type=MESH)

    def first_piece(g):
        return g * n_h + (n_l if g >= 2 else 0)

    def fill(k):
        load_lead(k).wait()

        @pl.when(z == 0)
        def _():
            for h in range(2):
                block = out[0, h * half:(h + 1) * half, k * CW:(k + 1) * CW]
                lane[y, pl.ds(first_piece(2 * k + h), n_h)] = block.reshape(n_h, PR, CW)

    fill(0)
    pl.semaphore_wait(barrier, 3 + has_up.astype(jnp.int32) + has_down.astype(jnp.int32))

    def remote(src, dst, ssem, rsem, there):
        return pltpu.make_async_remote_copy(
            src_ref=src, dst_ref=dst, send_sem=ssem, recv_sem=rsem, device_id=there, device_id_type=MESH)

    def z_copy(p):
        return remote(lane.at[y, p], lane.at[y, p], zs.at[p], zr.at[p], up)

    def y_copy(p):
        return remote(lane.at[y, p], lane.at[y, p], ys.at[p], yr.at[p], across)

    def y_arrival(p):
        return remote(lane.at[1 - y, p], lane.at[1 - y, p], ys.at[p], yr.at[p], across)

    def x_ref(ref, at, i):
        rows = pl.ds((1, 3, 0, 2)[i] * quarter, quarter) if i < 4 else pl.ds((i - 4) * half, half)
        return ref.at[i // 4, rows] if at is None else ref.at[at, i // 4, rows]

    def x_copy(i):
        return remote(x_ref(fac, None, i), x_ref(pan, c, i), xs.at[i], xr.at[i], far)

    def x_arrival(i):
        return remote(x_ref(fac, None, i), x_ref(pan, peer, i), xs.at[i], xr.at[i], far)

    def p_ref(at, i):
        return pan.at[at, i % 2] if i < 3 else pan.at[at, 1, pl.ds((i - 3) * half, half)]

    def p_copy(i):
        if i < 2:
            return remote(fac.at[i], pan.at[c, i], ps.at[i], pr.at[i], beside)
        return remote(p_ref(peer, i), p_ref(peer, i), ps.at[i], pr.at[i], beside)

    def p_arrival(i):
        at = partner if i < 2 else peer2
        return remote(p_ref(at, i), p_ref(at, i), ps.at[i], pr.at[i], beside)

    def t_copy(i):
        rows = pl.ds(pl.multiple_of(x * quarter + i * PR, PR), PR)
        return remote(pan.at[core, 0, rows], lane.at[0, l_at + i], ts.at[i], tr.at[i], across)

    def lx_copy(b):
        return remote(lane.at[b, pl.ds(l_at, n_l)], l10x.at[b], us.at[b], ur.at[b], far)

    def lp_copy(i, b):
        src = l10x.at[b] if i else lane.at[b, pl.ds(l_at, n_l)]
        return remote(src, l10p.at[i, b], ls.at[i, b], lr.at[i, b], beside)

    def relay(p):
        @pl.when(has_down)
        def _():
            z_copy(p).wait_recv()

        @pl.when(jnp.logical_and(jnp.logical_and(z == 0, has_up), p >= Z_WINDOW))
        def _():
            z_copy(p - Z_WINDOW).wait_send()

        @pl.when(has_up)
        def _():
            z_copy(p).start()

        @pl.when(jnp.logical_and(z == 0, p >= Y_WINDOW))
        def _():
            y_copy(p - Y_WINDOW).wait_send()

        y_copy(p).start()

    def relays(start, stop):
        @pl.loop(start, stop)
        def _(p):
            relay(p)

    x_copy(0).start()
    x_copy(1).start()
    p_copy(0).start()
    p_copy(1).start()
    relays(0, 4)
    for k in range(1, n_chunk):
        fill(k)
        relay(3 + k)

    @pl.when(r < 2)
    def _():
        out[0] = jnp.zeros_like(out[0])

    relay(7)
    x_copy(2).start()
    x_copy(3).start()

    def split_inverse(i, h):
        rows = slice(h * half, (h + 1) * half)
        ih[i, rows], il[i, rows] = split(invf[i, rows])

    inv_copy[0].wait()
    split_inverse(0, 0)
    relay(8)
    x_arrival(0).wait_recv()
    x_arrival(1).wait_recv()
    for copy in own:
        copy.wait()

    @pl.when(r == 1)
    def _():
        for e in range(n_l):
            t_copy(e).start()
        rows = pl.ds(pl.multiple_of(half + x * quarter, quarter), quarter)
        lane[1, pl.ds(l_at, n_l)] = pan[core, 0, rows].reshape(n_l, PR, CW)

    relay(9)
    split_inverse(0, 1)
    relay(10)
    inv_copy[1].wait()
    split_inverse(1, 0)
    relay(11)
    split_inverse(1, 1)
    relay(12)
    x_copy(4).start()
    relays(13, 16)

    @pl.when(r == 0)
    def _():
        for i in range(n_l):
            t_copy(i).wait_recv()

    relays(16, 19)
    x_arrival(2).wait_recv()
    x_arrival(3).wait_recv()
    p_copy(2).start()
    relays(19, 24)
    for i in range(n_l):
        y_arrival(l_at + i).wait_recv()
    for b in range(2):
        lp_copy(0, b).start()
        lx_copy(b).start()
    relays(24, 26)
    for i in range(3):
        p_arrival(i).wait_recv()

    at_row = lax.broadcasted_iota(jnp.int32, (half, CW), 0)
    at_col = lax.broadcasted_iota(jnp.int32, (half, CW), 1)
    minus_one = jnp.where(at_row == at_col, -1.0, 0.0).astype(jnp.float32)

    def panel(q, t):
        j, m = t // 2, t % 2
        value = pan[q, j, m * half:(m + 1) * half]
        if j:
            return value
        mine = minus_one if q % 2 == m else jnp.zeros_like(minus_one)
        solved = jnp.where(r == q // 2, mine, jnp.zeros_like(mine))
        return jnp.where(r < 2, solved, value)

    def triangle(i, parts):
        (ah, al), (bh, bl) = parts
        first = (dot3(ah, al, ih[i, :half, :half], il[i, :half, :half])
                 + dot3(bh, bl, ih[i, half:, :half], il[i, half:, :half]))
        return first, dot3(bh, bl, ih[i, half:, half:], il[i, half:, half:])

    def columns(e, b):
        return slice((2 * e + b) * quarter, (2 * e + b + 1) * quarter)

    def keep(t, b, products):
        rows = slice(t * half, (t + 1) * half)
        for h, value in enumerate(products):
            high, low = split(value)
            for e in range(2):
                part = slice(e * quarter, (e + 1) * quarter)
                mh[rows, columns(2 * h + e, b)] = high[:, part]
                ml[rows, columns(2 * h + e, b)] = low[:, part]

    def kept(ref, rows, h):
        return jnp.concatenate([ref[rows, columns(2 * h, 1)], ref[rows, columns(2 * h + 1, 1)]], axis=1)

    def second_factor(t):
        keep(t, 1, triangle(1, [split(panel(2, t)), split(panel(3, t))]))

    def first_factor(t):
        rows = slice(t * half, (t + 1) * half)
        parts = []
        for q in range(2):
            value = panel(q, t)
            for h in range(2):
                ks = slice(h * half, (h + 1) * half)
                value = value - dot3(kept(mh, rows, h), kept(ml, rows, h), lh[q, ks], ll[q, ks])
            parts.append(split(value))
        keep(t, 0, triangle(0, parts))

    second_factor(0)
    relay(26)
    second_factor(1)
    relay(27)
    x_arrival(4).wait_recv()
    p_copy(3).start()
    relay(28)
    x_copy(5).start()
    relays(29, 33)
    p_arrival(3).wait_recv()
    second_factor(2)
    relays(33, 36)
    for b in range(2):
        lx_copy(b).wait_recv()
        lp_copy(1, b).start()
    relays(36, 39)
    for b in range(2):
        lp_copy(0, b).wait_recv()
        lp_copy(1, b).wait_recv()
        for at, e, block in ((core, x, lane[b, pl.ds(l_at, n_l)]), (core, 1 - x, l10x[b]),
                             (1 - core, x, l10p[0, b]), (1 - core, 1 - x, l10p[1, b])):
            h, l = split(block.reshape(quarter, CW))
            rows = pl.ds(pl.multiple_of(b * half + e * quarter, quarter), quarter)
            lh[at, rows] = h
            ll[at, rows] = l
    load_rest.wait()
    for t in range(3):
        relay(39 + t)
        first_factor(t)
    relay(42)
    x_arrival(5).wait_recv()
    p_copy(4).start()
    relays(43, 46)
    p_arrival(4).wait_recv()
    second_factor(3)
    relay(46)
    first_factor(3)

    def gather(start, quarters):
        count = n_h // 2

        @pl.loop(start, start + quarters * count)
        def _(p):
            y_arrival(p).wait_recv()

        for e in range(quarters):
            for b in range(2):
                rows = slice((2 * e + b) * quarter, (2 * e + b + 1) * quarter)
                xh[rows], xl[rows] = split(lane[b, pl.ds(start + e * count, count)].reshape(quarter, CW))

    def update(k, t, ks, width):
        rows = pl.ds(pl.multiple_of(t * half, half), half)
        place = (t // 2, pl.ds(pl.multiple_of((t % 2) * half, half), half), pl.ds(pl.multiple_of(k * CW, CW), CW))
        out[place] = out[place] - dot3(mh[rows, ks], ml[rows, ks], xh[:width], xl[:width])

    last = 2 * n_chunk - 1

    @pl.loop(0, 4 * last)
    def _(n):
        g, t = n // 4, n % 4

        @pl.when(t < 3)
        def _():
            relay(47 + 3 * g + t)

        @pl.when(t == 0)
        def _():
            gather(g * n_h + jnp.where(g >= 2, n_l, 0), 2)

        update(g // 2, t, pl.ds(pl.multiple_of((g % 2) * nb, nb), nb), nb)

    for e in range(2):
        gather(first_piece(last) + e * (n_h // 2), 1)

        @pl.loop(0, 4)
        def _(t):
            update(n_chunk - 1, t, pl.ds(nb + e * half, half), half)

    for i in range(6):
        x_copy(i).wait_send()
    for i in range(5):
        p_copy(i).wait_send()
    for b in range(2):
        lx_copy(b).wait_send()
        lp_copy(0, b).wait_send()
        lp_copy(1, b).wait_send()

    @pl.when(r == 1)
    def _():
        for i in range(n_l):
            t_copy(i).wait_send()

    @pl.loop(jnp.where(z == 0, n_piece - Y_WINDOW, 0), n_piece)
    def _(p):
        y_copy(p).wait_send()

    @pl.when(has_up)
    def _():
        @pl.loop(jnp.where(z == 0, n_piece - Z_WINDOW, 0), n_piece)
        def _(p):
            z_copy(p).wait_send()


def shards(n_row, rhs, factor, inverses):
    nb = rhs.shape[1]
    n_chunk = rhs.shape[2] // CW
    ppc = nb // PR
    n_l = ppc // 4
    n_piece = n_chunk * ppc + n_l
    f32, bf16, dma = jnp.float32, jnp.bfloat16, pltpu.SemaphoreType.DMA
    anywhere = pl.BlockSpec(memory_space=pl.ANY)
    return pl.pallas_call(
        functools.partial(kernel, n_row),
        out_shape=pltpu.VMEM(rhs.shape, f32),
        in_specs=[anywhere] * 3,
        out_specs=pl.BlockSpec(memory_space=pltpu.VMEM),
        scratch_shapes=[
            pltpu.VMEM((2, n_piece, PR, CW), f32),
            pltpu.VMEM((4, 2, nb, CW), f32),
            pltpu.VMEM((2, 2, n_l, PR, CW), f32),
            pltpu.VMEM((2, n_l, PR, CW), f32),
            pltpu.VMEM((2, nb, nb), f32),
            pltpu.VMEM((2 * nb, 2 * nb), bf16),
            pltpu.VMEM((2 * nb, 2 * nb), bf16),
            pltpu.VMEM((2, nb, nb), bf16),
            pltpu.VMEM((2, nb, nb), bf16),
            pltpu.VMEM((2, nb, CW), bf16),
            pltpu.VMEM((2, nb, CW), bf16),
            pltpu.VMEM((nb, CW), bf16),
            pltpu.VMEM((nb, CW), bf16),
            dma((n_chunk + 1,)), dma((2,)), dma((2,)),
            dma((n_piece,)), dma((n_piece,)), dma((n_piece,)), dma((n_piece,)),
            dma((6,)), dma((6,)), dma((5,)), dma((5,)),
            dma((n_l,)), dma((n_l,)), dma((2, 2)), dma((2, 2)), dma((2,)), dma((2,)),
        ],
        compiler_params=pltpu.CompilerParams(
            collective_id=0, has_side_effects=True, vmem_limit_bytes=59 * 1024 * 1024),
        cost_estimate=pl.CostEstimate(flops=8 * 10 ** 9, bytes_accessed=12 * 2 ** 20, transcendentals=0),
    )(rhs, factor, inverses)


def solution(mesh):
    placed = (P(None, "row", "col"), P(None, "row", "col"), P())
    return jax.shard_map(
        functools.partial(shards, mesh.shape["row"]), mesh=mesh, in_specs=placed,
        out_specs=P(None, "row", "col"), check_vma=False)
```

```python
import functools

import jax
import jax.numpy as jnp
from jax import lax
from jax.experimental import pallas as pl
from jax.experimental.pallas import tpu as pltpu
from jax.sharding import PartitionSpec as P

MESH = pl.DeviceIdType.MESH
CW = 256
PR = 32
Z_WINDOW = 16
Y_WINDOW = 28


def split(value):
    high = value.astype(jnp.bfloat16)
    low = (value - high.astype(jnp.float32)).astype(jnp.bfloat16)
    return high, low


def dot3(ah, al, bh, bl):
    def one(a, b):
        return jnp.dot(a, b, preferred_element_type=jnp.float32)

    return one(ah, bh) + one(al, bh) + one(ah, bl)


def kernel(n_row, rhs, fac, inv, out, lane, pan, l10p, l10x, invf, mh, ml, ih, il, lh, ll, xh, xl,
           acc_sem, inv_sem, own_sem, zs, zr, ys, yr, xs, xr, ps, pr, ts, tr, ls, lr, us, ur):
    nb = rhs.shape[1]
    n_chunk = rhs.shape[2] // CW
    ppc = nb // PR
    n_h = ppc // 2
    n_l = ppc // 4
    n_piece = n_chunk * ppc + n_l
    l_at = 2 * n_h
    half, quarter = nb // 2, nb // 4

    r = lax.axis_index("row")
    c = lax.axis_index("col")
    z, y = r // 2, r % 2
    n_z = n_row // 2
    core, x = c % 2, c // 2
    partner = c + 1 - 2 * core
    peer = (c + 2) % 4
    peer2 = (partner + 2) % 4
    has_up = z < n_z - 1
    has_down = z > 0
    up, down, across = (r + 2, c), (r - 2, c), (r + 1 - 2 * y, c)
    beside, far = (r, partner), (r, peer)

    def load_lead(k):
        cols = pl.ds(k * CW, CW)
        return pltpu.make_async_copy(rhs.at[0, :, cols], out.at[0, :, cols], acc_sem.at[k])

    load_rest = pltpu.make_async_copy(rhs.at[1], out.at[1], acc_sem.at[n_chunk])
    own = [pltpu.make_async_copy(fac.at[j], pan.at[c, j], own_sem.at[j]) for j in range(2)]
    inv_copy = [pltpu.make_async_copy(inv.at[i], invf.at[i], inv_sem.at[i]) for i in range(2)]
    for k in range(n_chunk):
        load_lead(k).start()
    for copy in own + inv_copy + [load_rest]:
        copy.start()

    barrier = pltpu.get_barrier_semaphore()
    for there in (across, beside, far):
        pl.semaphore_signal(barrier, inc=1, device_id=there, device_id_type=MESH)

    @pl.when(has_up)
    def _():
        pl.semaphore_signal(barrier, inc=1, device_id=up, device_id_type=MESH)

    @pl.when(has_down)
    def _():
        pl.semaphore_signal(barrier, inc=1, device_id=down, device_id_type=MESH)

    def first_piece(g):
        return g * n_h + (n_l if g >= 2 else 0)

    def fill(k):
        load_lead(k).wait()

        @pl.when(z == 0)
        def _():
            for h in range(2):
                block = out[0, h * half:(h + 1) * half, k * CW:(k + 1) * CW]
                lane[y, pl.ds(first_piece(2 * k + h), n_h)] = block.reshape(n_h, PR, CW)

    fill(0)
    pl.semaphore_wait(barrier, 3 + has_up.astype(jnp.int32) + has_down.astype(jnp.int32))

    def remote(src, dst, ssem, rsem, there):
        return pltpu.make_async_remote_copy(
            src_ref=src, dst_ref=dst, send_sem=ssem, recv_sem=rsem, device_id=there, device_id_type=MESH)

    def z_copy(p):
        return remote(lane.at[y, p], lane.at[y, p], zs.at[p], zr.at[p], up)

    def y_copy(p):
        return remote(lane.at[y, p], lane.at[y, p], ys.at[p], yr.at[p], across)

    def y_arrival(p):
        return remote(lane.at[1 - y, p], lane.at[1 - y, p], ys.at[p], yr.at[p], across)

    def x_ref(ref, at, i):
        rows = pl.ds((1, 3, 0, 2)[i] * quarter, quarter) if i < 4 else pl.ds((i - 4) * half, half)
        return ref.at[i // 4, rows] if at is None else ref.at[at, i // 4, rows]

    def x_copy(i):
        return remote(x_ref(fac, None, i), x_ref(pan, c, i), xs.at[i], xr.at[i], far)

    def x_arrival(i):
        return remote(x_ref(fac, None, i), x_ref(pan, peer, i), xs.at[i], xr.at[i], far)

    def p_ref(at, i):
        return pan.at[at, i % 2] if i < 3 else pan.at[at, 1, pl.ds((i - 3) * half, half)]

    def p_copy(i):
        if i < 2:
            return remote(fac.at[i], pan.at[c, i], ps.at[i], pr.at[i], beside)
        return remote(p_ref(peer, i), p_ref(peer, i), ps.at[i], pr.at[i], beside)

    def p_arrival(i):
        at = partner if i < 2 else peer2
        return remote(p_ref(at, i), p_ref(at, i), ps.at[i], pr.at[i], beside)

    def t_copy(i):
        rows = pl.ds(pl.multiple_of(x * quarter + i * PR, PR), PR)
        return remote(pan.at[core, 0, rows], lane.at[0, l_at + i], ts.at[i], tr.at[i], across)

    def lx_copy(b):
        return remote(lane.at[b, pl.ds(l_at, n_l)], l10x.at[b], us.at[b], ur.at[b], far)

    def lp_copy(i, b):
        src = l10x.at[b] if i else lane.at[b, pl.ds(l_at, n_l)]
        return remote(src, l10p.at[i, b], ls.at[i, b], lr.at[i, b], beside)

    def relay(p):
        @pl.when(has_down)
        def _():
            z_copy(p).wait_recv()

        @pl.when(jnp.logical_and(jnp.logical_and(z == 0, has_up), p >= Z_WINDOW))
        def _():
            z_copy(p - Z_WINDOW).wait_send()

        @pl.when(has_up)
        def _():
            z_copy(p).start()

        @pl.when(jnp.logical_and(z == 0, p >= Y_WINDOW))
        def _():
            y_copy(p - Y_WINDOW).wait_send()

        y_copy(p).start()

    def relays(start, stop):
        @pl.loop(start, stop)
        def _(p):
            relay(p)

    x_copy(0).start()
    x_copy(1).start()
    p_copy(0).start()
    p_copy(1).start()
    relays(0, 4)
    for k in range(1, n_chunk):
        fill(k)
        relay(3 + k)

    @pl.when(r < 2)
    def _():
        out[0] = jnp.zeros_like(out[0])

    relay(7)
    x_copy(2).start()
    x_copy(3).start()

    def split_inverse(i, h):
        rows = slice(h * half, (h + 1) * half)
        ih[i, rows], il[i, rows] = split(invf[i, rows])

    inv_copy[0].wait()
    split_inverse(0, 0)
    relay(8)
    x_arrival(0).wait_recv()
    x_arrival(1).wait_recv()
    for copy in own:
        copy.wait()

    @pl.when(r == 1)
    def _():
        for e in range(n_l):
            t_copy(e).start()
        rows = pl.ds(pl.multiple_of(half + x * quarter, quarter), quarter)
        lane[1, pl.ds(l_at, n_l)] = pan[core, 0, rows].reshape(n_l, PR, CW)

    relay(9)
    split_inverse(0, 1)
    relay(10)
    inv_copy[1].wait()
    split_inverse(1, 0)
    relay(11)
    split_inverse(1, 1)
    relay(12)
    x_copy(4).start()
    relays(13, 16)

    @pl.when(r == 0)
    def _():
        for i in range(n_l):
            t_copy(i).wait_recv()

    relays(16, 22)
    x_arrival(2).wait_recv()
    x_arrival(3).wait_recv()
    p_copy(2).start()
    relays(22, 24)
    for i in range(n_l):
        y_arrival(l_at + i).wait_recv()
    for b in range(2):
        lp_copy(0, b).start()
        lx_copy(b).start()
    x_copy(5).start()
    relays(24, 29)
    for i in range(3):
        p_arrival(i).wait_recv()

    at_row = lax.broadcasted_iota(jnp.int32, (half, CW), 0)
    at_col = lax.broadcasted_iota(jnp.int32, (half, CW), 1)
    minus_one = jnp.where(at_row == at_col, -1.0, 0.0).astype(jnp.float32)

    def panel(q, t):
        j, m = t // 2, t % 2
        value = pan[q, j, m * half:(m + 1) * half]
        if j:
            return value
        mine = minus_one if q % 2 == m else jnp.zeros_like(minus_one)
        solved = jnp.where(r == q // 2, mine, jnp.zeros_like(mine))
        return jnp.where(r < 2, solved, value)

    def triangle(i, parts):
        (ah, al), (bh, bl) = parts
        first = (dot3(ah, al, ih[i, :half, :half], il[i, :half, :half])
                 + dot3(bh, bl, ih[i, half:, :half], il[i, half:, :half]))
        return first, dot3(bh, bl, ih[i, half:, half:], il[i, half:, half:])

    def columns(e, b):
        return slice((2 * e + b) * quarter, (2 * e + b + 1) * quarter)

    def keep(t, b, products):
        rows = slice(t * half, (t + 1) * half)
        for h, value in enumerate(products):
            high, low = split(value)
            for e in range(2):
                part = slice(e * quarter, (e + 1) * quarter)
                mh[rows, columns(2 * h + e, b)] = high[:, part]
                ml[rows, columns(2 * h + e, b)] = low[:, part]

    def kept(ref, rows, h):
        return jnp.concatenate([ref[rows, columns(2 * h, 1)], ref[rows, columns(2 * h + 1, 1)]], axis=1)

    def second_factor(t):
        keep(t, 1, triangle(1, [split(panel(2, t)), split(panel(3, t))]))

    def first_factor(t):
        rows = slice(t * half, (t + 1) * half)
        parts = []
        for q in range(2):
            value = panel(q, t)
            for h in range(2):
                ks = slice(h * half, (h + 1) * half)
                value = value - dot3(kept(mh, rows, h), kept(ml, rows, h), lh[q, ks], ll[q, ks])
            parts.append(split(value))
        keep(t, 0, triangle(0, parts))

    second_factor(0)
    relay(29)
    second_factor(1)
    relays(30, 32)
    x_arrival(4).wait_recv()
    p_copy(3).start()
    relays(32, 36)
    p_arrival(3).wait_recv()
    second_factor(2)
    relays(36, 38)
    for b in range(2):
        lx_copy(b).wait_recv()
        lp_copy(1, b).start()
    relays(38, 41)
    for b in range(2):
        lp_copy(0, b).wait_recv()
        lp_copy(1, b).wait_recv()
        for at, e, block in ((core, x, lane[b, pl.ds(l_at, n_l)]), (core, 1 - x, l10x[b]),
                             (1 - core, x, l10p[0, b]), (1 - core, 1 - x, l10p[1, b])):
            h, l = split(block.reshape(quarter, CW))
            rows = pl.ds(pl.multiple_of(b * half + e * quarter, quarter), quarter)
            lh[at, rows] = h
            ll[at, rows] = l
    load_rest.wait()
    for t in range(3):
        relay(41 + t)
        first_factor(t)
    relays(44, 46)
    x_arrival(5).wait_recv()
    p_copy(4).start()
    relays(46, 49)
    p_arrival(4).wait_recv()
    second_factor(3)
    relay(49)
    first_factor(3)

    def gather(start, quarters):
        count = n_h // 2

        @pl.loop(start, start + quarters * count)
        def _(p):
            y_arrival(p).wait_recv()

        for e in range(quarters):
            for b in range(2):
                rows = slice((2 * e + b) * quarter, (2 * e + b + 1) * quarter)
                xh[rows], xl[rows] = split(lane[b, pl.ds(start + e * count, count)].reshape(quarter, CW))

    def update(k, t, ks, width):
        rows = pl.ds(pl.multiple_of(t * half, half), half)
        place = (t // 2, pl.ds(pl.multiple_of((t % 2) * half, half), half), pl.ds(pl.multiple_of(k * CW, CW), CW))
        out[place] = out[place] - dot3(mh[rows, ks], ml[rows, ks], xh[:width], xl[:width])

    last = 2 * n_chunk - 1

    @pl.loop(0, 4 * last)
    def _(n):
        g, t = n // 4, n % 4

        @pl.when(t < jnp.where(g < 4, 3, 2))
        def _():
            relay(50 + 3 * g - jnp.maximum(g - 4, 0) + t)

        @pl.when(t == 0)
        def _():
            gather(g * n_h + jnp.where(g >= 2, n_l, 0), 2)

        update(g // 2, t, pl.ds(pl.multiple_of((g % 2) * nb, nb), nb), nb)

    for e in range(2):
        gather(first_piece(last) + e * (n_h // 2), 1)

        @pl.loop(0, 4)
        def _(t):
            update(n_chunk - 1, t, pl.ds(nb + e * half, half), half)

    for i in range(6):
        x_copy(i).wait_send()
    for i in range(5):
        p_copy(i).wait_send()
    for b in range(2):
        lx_copy(b).wait_send()
        lp_copy(0, b).wait_send()
        lp_copy(1, b).wait_send()

    @pl.when(r == 1)
    def _():
        for i in range(n_l):
            t_copy(i).wait_send()

    @pl.loop(jnp.where(z == 0, n_piece - Y_WINDOW, 0), n_piece)
    def _(p):
        y_copy(p).wait_send()

    @pl.when(has_up)
    def _():
        @pl.loop(jnp.where(z == 0, n_piece - Z_WINDOW, 0), n_piece)
        def _(p):
            z_copy(p).wait_send()


def shards(n_row, rhs, factor, inverses):
    nb = rhs.shape[1]
    n_chunk = rhs.shape[2] // CW
    ppc = nb // PR
    n_l = ppc // 4
    n_piece = n_chunk * ppc + n_l
    f32, bf16, dma = jnp.float32, jnp.bfloat16, pltpu.SemaphoreType.DMA
    anywhere = pl.BlockSpec(memory_space=pl.ANY)
    return pl.pallas_call(
        functools.partial(kernel, n_row),
        out_shape=pltpu.VMEM(rhs.shape, f32),
        in_specs=[anywhere] * 3,
        out_specs=pl.BlockSpec(memory_space=pltpu.VMEM),
        scratch_shapes=[
            pltpu.VMEM((2, n_piece, PR, CW), f32),
            pltpu.VMEM((4, 2, nb, CW), f32),
            pltpu.VMEM((2, 2, n_l, PR, CW), f32),
            pltpu.VMEM((2, n_l, PR, CW), f32),
            pltpu.VMEM((2, nb, nb), f32),
            pltpu.VMEM((2 * nb, 2 * nb), bf16),
            pltpu.VMEM((2 * nb, 2 * nb), bf16),
            pltpu.VMEM((2, nb, nb), bf16),
            pltpu.VMEM((2, nb, nb), bf16),
            pltpu.VMEM((2, nb, CW), bf16),
            pltpu.VMEM((2, nb, CW), bf16),
            pltpu.VMEM((nb, CW), bf16),
            pltpu.VMEM((nb, CW), bf16),
            dma((n_chunk + 1,)), dma((2,)), dma((2,)),
            dma((n_piece,)), dma((n_piece,)), dma((n_piece,)), dma((n_piece,)),
            dma((6,)), dma((6,)), dma((5,)), dma((5,)),
            dma((n_l,)), dma((n_l,)), dma((2, 2)), dma((2, 2)), dma((2,)), dma((2,)),
        ],
        compiler_params=pltpu.CompilerParams(
            collective_id=0, has_side_effects=True, vmem_limit_bytes=59 * 1024 * 1024),
        cost_estimate=pl.CostEstimate(flops=8 * 10 ** 9, bytes_accessed=12 * 2 ** 20, transcendentals=0),
    )(rhs, factor, inverses)


def solution(mesh):
    placed = (P(None, "row", "col"), P(None, "row", "col"), P())
    return jax.shard_map(
        functools.partial(shards, mesh.shape["row"]), mesh=mesh, in_specs=placed,
        out_specs=P(None, "row", "col"), check_vma=False)
```

```python
import functools

import jax
import jax.numpy as jnp
from jax import lax
from jax.experimental import pallas as pl
from jax.experimental.pallas import tpu as pltpu
from jax.sharding import PartitionSpec as P

MESH = pl.DeviceIdType.MESH
CW = 256
PR = 32
Z_WINDOW = 16
Y_WINDOW = 28


def split(value):
    high = value.astype(jnp.bfloat16)
    low = (value - high.astype(jnp.float32)).astype(jnp.bfloat16)
    return high, low


def dot3(ah, al, bh, bl):
    def one(a, b):
        return jnp.dot(a, b, preferred_element_type=jnp.float32)

    return one(ah, bh) + one(al, bh) + one(ah, bl)


def kernel(n_row, rhs, fac, inv, out, lane, pan, l10p, l10x, invf, mh, ml, ih, il, lh, ll, xh, xl,
           acc_sem, inv_sem, own_sem, zs, zr, ys, yr, xs, xr, ps, pr, ts, tr, ls, lr, us, ur,
           zs2, zr2, ys2, yr2):
    nb = rhs.shape[1]
    n_chunk = rhs.shape[2] // CW
    ppc = nb // PR
    n_h = ppc // 2
    n_l = ppc // 4
    n_piece = n_chunk * ppc + n_l
    l_at = 2 * n_h
    n_main = n_piece - n_h
    half, quarter = nb // 2, nb // 4

    r = lax.axis_index("row")
    c = lax.axis_index("col")
    z, y = r // 2, r % 2
    n_z = n_row // 2
    core, x = c % 2, c // 2
    partner = c + 1 - 2 * core
    peer = (c + 2) % 4
    peer2 = (partner + 2) % 4
    has_up = z < n_z - 1
    has_down = z > 0
    up, down, across = (r + 2, c), (r - 2, c), (r + 1 - 2 * y, c)
    beside, far = (r, partner), (r, peer)

    def load_lead(k):
        cols = pl.ds(k * CW, CW)
        return pltpu.make_async_copy(rhs.at[0, :, cols], out.at[0, :, cols], acc_sem.at[k])

    load_rest = pltpu.make_async_copy(rhs.at[1], out.at[1], acc_sem.at[n_chunk])
    own = [pltpu.make_async_copy(fac.at[j], pan.at[c, j], own_sem.at[j]) for j in range(2)]
    inv_copy = [pltpu.make_async_copy(inv.at[i], invf.at[i], inv_sem.at[i]) for i in range(2)]
    for k in range(n_chunk):
        load_lead(k).start()
    for copy in own + inv_copy + [load_rest]:
        copy.start()

    barrier = pltpu.get_barrier_semaphore()
    for there in (across, beside, far):
        pl.semaphore_signal(barrier, inc=1, device_id=there, device_id_type=MESH)

    @pl.when(has_up)
    def _():
        pl.semaphore_signal(barrier, inc=1, device_id=up, device_id_type=MESH)

    @pl.when(has_down)
    def _():
        pl.semaphore_signal(barrier, inc=1, device_id=down, device_id_type=MESH)

    def first_piece(g):
        return g * n_h + (n_l if g >= 2 else 0)

    def fill(k):
        load_lead(k).wait()

        @pl.when(z == 0)
        def _():
            for h in range(2):
                block = out[0, h * half:(h + 1) * half, k * CW:(k + 1) * CW]
                lane[y, pl.ds(first_piece(2 * k + h), n_h)] = block.reshape(n_h, PR, CW)

    fill(0)
    pl.semaphore_wait(barrier, 3 + has_up.astype(jnp.int32) + has_down.astype(jnp.int32))

    def remote(src, dst, ssem, rsem, there):
        return pltpu.make_async_remote_copy(
            src_ref=src, dst_ref=dst, send_sem=ssem, recv_sem=rsem, device_id=there, device_id_type=MESH)

    def z_copy(p):
        return remote(lane.at[y, p], lane.at[y, p], zs.at[p], zr.at[p], up)

    def y_copy(p):
        return remote(lane.at[y, p], lane.at[y, p], ys.at[p], yr.at[p], across)

    def y_arrival(p):
        return remote(lane.at[1 - y, p], lane.at[1 - y, p], ys.at[p], yr.at[p], across)

    def x_ref(ref, at, i):
        rows = pl.ds((1, 3, 0, 2)[i] * quarter, quarter) if i < 4 else pl.ds((i - 4) * half, half)
        return ref.at[i // 4, rows] if at is None else ref.at[at, i // 4, rows]

    def x_copy(i):
        return remote(x_ref(fac, None, i), x_ref(pan, c, i), xs.at[i], xr.at[i], far)

    def x_arrival(i):
        return remote(x_ref(fac, None, i), x_ref(pan, peer, i), xs.at[i], xr.at[i], far)

    def p_ref(at, i):
        return pan.at[at, i % 2] if i < 3 else pan.at[at, 1, pl.ds((i - 3) * half, half)]

    def p_copy(i):
        if i < 2:
            return remote(fac.at[i], pan.at[c, i], ps.at[i], pr.at[i], beside)
        return remote(p_ref(peer, i), p_ref(peer, i), ps.at[i], pr.at[i], beside)

    def p_arrival(i):
        at = partner if i < 2 else peer2
        return remote(p_ref(at, i), p_ref(at, i), ps.at[i], pr.at[i], beside)

    def t_copy(i):
        rows = pl.ds(pl.multiple_of(x * quarter + i * PR, PR), PR)
        return remote(pan.at[core, 0, rows], lane.at[0, l_at + i], ts.at[i], tr.at[i], across)

    def lx_copy(b):
        return remote(lane.at[b, pl.ds(l_at, n_l)], l10x.at[b], us.at[b], ur.at[b], far)

    def lp_copy(i, b):
        src = l10x.at[b] if i else lane.at[b, pl.ds(l_at, n_l)]
        return remote(src, l10p.at[i, b], ls.at[i, b], lr.at[i, b], beside)

    def relay(p):
        @pl.when(has_down)
        def _():
            z_copy(p).wait_recv()

        @pl.when(jnp.logical_and(jnp.logical_and(z == 0, has_up), p >= Z_WINDOW))
        def _():
            z_copy(p - Z_WINDOW).wait_send()

        @pl.when(has_up)
        def _():
            z_copy(p).start()

        @pl.when(jnp.logical_and(z == 0, p >= Y_WINDOW))
        def _():
            y_copy(p - Y_WINDOW).wait_send()

        y_copy(p).start()

    def fine(b, i):
        return lane.at[b, n_main + i // 2, pl.ds(pl.multiple_of((i % 2) * (PR // 2), PR // 2), PR // 2)]

    def z_fine(i):
        return remote(fine(y, i), fine(y, i), zs2.at[i], zr2.at[i], up)

    def y_fine(i):
        return remote(fine(y, i), fine(y, i), ys2.at[i], yr2.at[i], across)

    def y_fine_arrival(i):
        return remote(fine(1 - y, i), fine(1 - y, i), ys2.at[i], yr2.at[i], across)

    def relay_fine(i):
        @pl.when(has_down)
        def _():
            z_fine(i).wait_recv()

        @pl.when(has_up)
        def _():
            z_fine(i).start()

        y_fine(i).start()

    def relays(start, stop):
        @pl.loop(start, stop)
        def _(p):
            relay(p)

    x_copy(0).start()
    x_copy(1).start()
    p_copy(0).start()
    p_copy(1).start()
    relays(0, 4)
    for k in range(1, n_chunk):
        fill(k)
        relay(3 + k)

    @pl.when(r < 2)
    def _():
        out[0] = jnp.zeros_like(out[0])

    relay(7)
    x_copy(2).start()
    x_copy(3).start()

    def split_inverse(i, h):
        rows = slice(h * half, (h + 1) * half)
        ih[i, rows], il[i, rows] = split(invf[i, rows])

    inv_copy[0].wait()
    split_inverse(0, 0)
    relay(8)
    x_arrival(0).wait_recv()
    x_arrival(1).wait_recv()
    for copy in own:
        copy.wait()

    @pl.when(r == 1)
    def _():
        for e in range(n_l):
            t_copy(e).start()
        rows = pl.ds(pl.multiple_of(half + x * quarter, quarter), quarter)
        lane[1, pl.ds(l_at, n_l)] = pan[core, 0, rows].reshape(n_l, PR, CW)

    relay(9)
    split_inverse(0, 1)
    relay(10)
    inv_copy[1].wait()
    split_inverse(1, 0)
    relay(11)
    split_inverse(1, 1)
    relay(12)
    x_copy(4).start()
    relays(13, 16)

    @pl.when(r == 0)
    def _():
        for i in range(n_l):
            t_copy(i).wait_recv()

    relays(16, 19)
    x_arrival(2).wait_recv()
    x_arrival(3).wait_recv()
    p_copy(2).start()
    relays(19, 24)
    for i in range(n_l):
        y_arrival(l_at + i).wait_recv()
    for b in range(2):
        lp_copy(0, b).start()
        lx_copy(b).start()
    relays(24, 26)
    for i in range(3):
        p_arrival(i).wait_recv()

    at_row = lax.broadcasted_iota(jnp.int32, (half, CW), 0)
    at_col = lax.broadcasted_iota(jnp.int32, (half, CW), 1)
    minus_one = jnp.where(at_row == at_col, -1.0, 0.0).astype(jnp.float32)

    def panel(q, t):
        j, m = t // 2, t % 2
        value = pan[q, j, m * half:(m + 1) * half]
        if j:
            return value
        mine = minus_one if q % 2 == m else jnp.zeros_like(minus_one)
        solved = jnp.where(r == q // 2, mine, jnp.zeros_like(mine))
        return jnp.where(r < 2, solved, value)

    def triangle(i, parts):
        (ah, al), (bh, bl) = parts
        first = (dot3(ah, al, ih[i, :half, :half], il[i, :half, :half])
                 + dot3(bh, bl, ih[i, half:, :half], il[i, half:, :half]))
        return first, dot3(bh, bl, ih[i, half:, half:], il[i, half:, half:])

    def columns(e, b):
        return slice((2 * e + b) * quarter, (2 * e + b + 1) * quarter)

    def keep(t, b, products):
        rows = slice(t * half, (t + 1) * half)
        for h, value in enumerate(products):
            high, low = split(value)
            for e in range(2):
                part = slice(e * quarter, (e + 1) * quarter)
                mh[rows, columns(2 * h + e, b)] = high[:, part]
                ml[rows, columns(2 * h + e, b)] = low[:, part]

    def kept(ref, rows, h):
        return jnp.concatenate([ref[rows, columns(2 * h, 1)], ref[rows, columns(2 * h + 1, 1)]], axis=1)

    def second_factor(t):
        keep(t, 1, triangle(1, [split(panel(2, t)), split(panel(3, t))]))

    def first_factor(t):
        rows = slice(t * half, (t + 1) * half)
        parts = []
        for q in range(2):
            value = panel(q, t)
            for h in range(2):
                ks = slice(h * half, (h + 1) * half)
                value = value - dot3(kept(mh, rows, h), kept(ml, rows, h), lh[q, ks], ll[q, ks])
            parts.append(split(value))
        keep(t, 0, triangle(0, parts))

    second_factor(0)
    relay(26)
    second_factor(1)
    relay(27)
    x_arrival(4).wait_recv()
    p_copy(3).start()
    relay(28)
    x_copy(5).start()
    relays(29, 33)
    p_arrival(3).wait_recv()
    second_factor(2)
    relays(33, 36)
    for b in range(2):
        lx_copy(b).wait_recv()
        lp_copy(1, b).start()
    relays(36, 39)
    for b in range(2):
        lp_copy(0, b).wait_recv()
        lp_copy(1, b).wait_recv()
        for at, e, block in ((core, x, lane[b, pl.ds(l_at, n_l)]), (core, 1 - x, l10x[b]),
                             (1 - core, x, l10p[0, b]), (1 - core, 1 - x, l10p[1, b])):
            h, l = split(block.reshape(quarter, CW))
            rows = pl.ds(pl.multiple_of(b * half + e * quarter, quarter), quarter)
            lh[at, rows] = h
            ll[at, rows] = l
    load_rest.wait()
    for t in range(3):
        relay(39 + t)
        first_factor(t)
    relay(42)
    x_arrival(5).wait_recv()
    p_copy(4).start()
    relays(43, 46)
    p_arrival(4).wait_recv()
    second_factor(3)
    relay(46)
    first_factor(3)

    def gather(start, quarters):
        count = n_h // 2

        for e in range(quarters):
            for b in range(2):
                rows = slice((2 * e + b) * quarter, (2 * e + b + 1) * quarter)
                xh[rows], xl[rows] = split(lane[b, pl.ds(start + e * count, count)].reshape(quarter, CW))

    def update(k, t, ks, width):
        rows = pl.ds(pl.multiple_of(t * half, half), half)
        place = (t // 2, pl.ds(pl.multiple_of((t % 2) * half, half), half), pl.ds(pl.multiple_of(k * CW, CW), CW))
        out[place] = out[place] - dot3(mh[rows, ks], ml[rows, ks], xh[:width], xl[:width])

    last = 2 * n_chunk - 1

    @pl.loop(0, 4 * last)
    def _(n):
        g, t = n // 4, n % 4

        @pl.when(n < 13)
        def _():
            relay(47 + n)

        @pl.when(n >= 13)
        def _():
            relay_fine(n - 13)

        @pl.when(t == 0)
        def _():
            start = g * n_h + jnp.where(g >= 2, n_l, 0)

            @pl.loop(start, start + n_h)
            def _(p):
                y_arrival(p).wait_recv()

            gather(start, 2)

        update(g // 2, t, pl.ds(pl.multiple_of((g % 2) * nb, nb), nb), nb)

    relay_fine(15)

    for e in range(2):
        @pl.loop(e * n_h, (e + 1) * n_h)
        def _(i):
            y_fine_arrival(i).wait_recv()

        gather(first_piece(last) + e * (n_h // 2), 1)

        @pl.loop(0, 4)
        def _(t):
            update(n_chunk - 1, t, pl.ds(nb + e * half, half), half)

    for i in range(6):
        x_copy(i).wait_send()
    for i in range(5):
        p_copy(i).wait_send()
    for b in range(2):
        lx_copy(b).wait_send()
        lp_copy(0, b).wait_send()
        lp_copy(1, b).wait_send()

    @pl.when(r == 1)
    def _():
        for i in range(n_l):
            t_copy(i).wait_send()

    @pl.loop(jnp.where(z == 0, n_main - Y_WINDOW, 0), n_main)
    def _(p):
        y_copy(p).wait_send()

    @pl.loop(0, 2 * n_h)
    def _(i):
        y_fine(i).wait_send()

    @pl.when(has_up)
    def _():
        @pl.loop(jnp.where(z == 0, n_main - Z_WINDOW, 0), n_main)
        def _(p):
            z_copy(p).wait_send()

        @pl.loop(0, 2 * n_h)
        def _(i):
            z_fine(i).wait_send()


def shards(n_row, rhs, factor, inverses):
    nb = rhs.shape[1]
    n_chunk = rhs.shape[2] // CW
    ppc = nb // PR
    n_l = ppc // 4
    n_piece = n_chunk * ppc + n_l
    f32, bf16, dma = jnp.float32, jnp.bfloat16, pltpu.SemaphoreType.DMA
    anywhere = pl.BlockSpec(memory_space=pl.ANY)
    return pl.pallas_call(
        functools.partial(kernel, n_row),
        out_shape=pltpu.VMEM(rhs.shape, f32),
        in_specs=[anywhere] * 3,
        out_specs=pl.BlockSpec(memory_space=pltpu.VMEM),
        scratch_shapes=[
            pltpu.VMEM((2, n_piece, PR, CW), f32),
            pltpu.VMEM((4, 2, nb, CW), f32),
            pltpu.VMEM((2, 2, n_l, PR, CW), f32),
            pltpu.VMEM((2, n_l, PR, CW), f32),
            pltpu.VMEM((2, nb, nb), f32),
            pltpu.VMEM((2 * nb, 2 * nb), bf16),
            pltpu.VMEM((2 * nb, 2 * nb), bf16),
            pltpu.VMEM((2, nb, nb), bf16),
            pltpu.VMEM((2, nb, nb), bf16),
            pltpu.VMEM((2, nb, CW), bf16),
            pltpu.VMEM((2, nb, CW), bf16),
            pltpu.VMEM((nb, CW), bf16),
            pltpu.VMEM((nb, CW), bf16),
            dma((n_chunk + 1,)), dma((2,)), dma((2,)),
            dma((n_piece,)), dma((n_piece,)), dma((n_piece,)), dma((n_piece,)),
            dma((6,)), dma((6,)), dma((5,)), dma((5,)),
            dma((n_l,)), dma((n_l,)), dma((2, 2)), dma((2, 2)), dma((2,)), dma((2,)),
            dma((ppc,)), dma((ppc,)), dma((ppc,)), dma((ppc,)),
        ],
        compiler_params=pltpu.CompilerParams(
            collective_id=0, has_side_effects=True, vmem_limit_bytes=59 * 1024 * 1024),
        cost_estimate=pl.CostEstimate(flops=8 * 10 ** 9, bytes_accessed=12 * 2 ** 20, transcendentals=0),
    )(rhs, factor, inverses)


def solution(mesh):
    placed = (P(None, "row", "col"), P(None, "row", "col"), P())
    return jax.shard_map(
        functools.partial(shards, mesh.shape["row"]), mesh=mesh, in_specs=placed,
        out_specs=P(None, "row", "col"), check_vma=False)
```
